32 devices in a mesh: term: 8 (over z, y), sector: 4 (over x, core).
Axes of the slice: x: 2, y: 2, z: 4, core: 2. Of those that a mesh axis runs over, the one named last changes fastest.
Arguments:
- wavefunction: bfloat16 [512, 128, 128], P(('term', 'sector')), may hold values from -6 to 6
- left_sector: int32 [512, 1], P(('term', 'sector')), may hold values from 0 to 3; in each aligned block of 16 rows (0 to 15, 16 to 31, ...) at most 8 rows name the same one
- right_sector: int32 [512], P(('term', 'sector')), may hold values from 0 to 3
- left_blocks: bfloat16 [16, 4, 128, 128], P('term', 'sector'), may hold values from -0.5 to 0.5
- right_blocks: bfloat16 [16, 4, 128, 128], P('term'), may hold values from -0.125 to 0.125
Outputs:
- product_blocks: bfloat16 [512, 128, 128], P(('term', 'sector'))
The draws below stay inside these ranges and needn't reach their ends.
Inputs may be any that keep to these rules, and one draw needn't show every extreme that they name: `left_sector`: among the 16 blocks of one device no left sector is named more than 8 times, and some left sector is named exactly 8 times.
All inputs are finite; a program needn't handle non-finite values.
Results may differ from the reference program's by a relative error of at most 0.0049.
Values may be sent and summed in bfloat16 or wider, within the bound.
No kernel may reach another device: no remote copies, remote signals or barrier semaphores. Data moves between devices by JAX's collectives and lax.ppermute only.
A program may use at most 64 MiB of HBM per device.

```python
import math
import jax
import jax.numpy as jnp
import numpy as np
from jax import lax

BLOCK = 128
BLK_DEV = 16
TERM_DEV = 2
RSEC = 4
CAP = 8
TERMS = 16
NBLK = 512
N_TERM = 8
N_SECTOR = 4


def set_ends(result, rng, least, largest):
    shape = result.shape
    index_at = [jax.random.randint(jax.random.fold_in(rng, axis), (), 0, shape[axis]) for axis in range(len(shape))]
    result = result.at[tuple(index_at)].set(least)
    longest = shape.index(max(shape))
    index_at[longest] = (index_at[longest] + 1) % shape[longest]
    return result.at[tuple(index_at)].set(largest)


def block_scale(rng, shape, split, least, top_value):
    factor_of, own = 1.0, jax.random.fold_in(rng, 6)
    for position, blocks in split:
        heights = jnp.exp(jax.random.uniform(jax.random.fold_in(own, position), (blocks,), jnp.float32, least / len(split), top_value / len(split)))
        factor_of = factor_of * jnp.repeat(heights, shape[position] // blocks).reshape([-1 if axis == position else 1 for axis in range(len(shape))])
    return factor_of


def deal_out(own_key, own, number, rows, amount, top, limit, skew):
    sequence = jax.random.permutation(own_key, amount)
    crowded, ordinary = portions_of(amount, rows * top, limit, skew, True), portions_of(amount, rows * top, limit, skew, False)
    places = jnp.arange(amount)

    def named(lengths, rotation):
        used = int((lengths > 0).sum())
        fixed = max(1, used // 4)
        passed = fixed + (places - fixed + rotation * (used - fixed)) % max(1, amount - fixed)
        return jnp.zeros((amount,), jnp.int32).at[sequence[jnp.where(places < fixed, places, passed)]].set(jnp.asarray(lengths, jnp.int32))

    lengths = jnp.where(number % 4 == 0, named(crowded, number // 4), named(ordinary, number - number // 4 - 1))
    mixed = jax.random.permutation(jax.random.fold_in(own, 3), amount)
    source_of, sink = mixed[0:amount // 2 * 2:2], mixed[1:amount // 2 * 2:2]
    margin = jnp.minimum(lengths[source_of] - 1, limit - lengths[sink]) // 2
    margin = jnp.where((source_of == sequence[0]) | (sink == sequence[0]) | (lengths[sink] == 0), 0, jnp.maximum(margin, 0))
    passed = jax.random.randint(jax.random.fold_in(own, 4), (amount // 2,), 0, 1 << 20) % (margin + 1)
    lengths = lengths.at[source_of].add(-passed).at[sink].add(passed)
    members = jnp.searchsorted(jnp.cumsum(lengths), jnp.arange(rows * top), side="right").astype(jnp.int32)
    table = members.reshape(top, rows).T
    table = table[jax.random.permutation(jax.random.fold_in(own, 1), rows)]
    rotation = jax.random.randint(jax.random.fold_in(own, 2), (rows, 1), 0, top)
    return jnp.take_along_axis(table, (jnp.arange(top)[None, :] + rotation) % top, axis=1)


def portions_of(count, total, bound, slope, full):
    loads = [(1 << 20) // math.isqrt(standing ** slope) + 1 for standing in range(1, count + 1)]
    largest = bound if full else min(bound, max(-(-total // count), total * loads[0] // sum(loads)))
    least = 1 if total - largest >= count - 1 else 0
    holding, spare = [largest] + [least] * (count - 1), total - largest - least * (count - 1)
    while spare > 0:
        candidates = [i for i in range(1, count) if holding[i] < largest] or [i for i in range(1, count) if holding[i] < bound]
        whole, budget = sum([loads[i] for i in candidates]), spare
        for i in candidates:
            addition = min(bound - holding[i], max(1, budget * loads[i] // whole), spare)
            holding[i] = holding[i] + addition
            spare = spare - addition
    return np.array(holding)


def noise(key, extent, deviation, limit, split=(), held_as=jnp.bfloat16):
    entries = deviation * jax.random.normal(key, extent, jnp.float32)
    if split:
        entries = entries * block_scale(key, extent, split, -0.22, 0.18)
    return jnp.clip(entries, -limit, limit).astype(held_as)


def setup_inputs(seed: int = 0) -> dict:
    keys = jax.random.split(jax.random.key(seed), 6)
    wavefunction = noise(keys[0], (NBLK, BLOCK, BLOCK), 1.0, 6.0, ((0, 32),))
    left_sector_keys = jax.random.split(jax.random.fold_in(keys[1], 1), NBLK // BLK_DEV)
    left_sector_turns = jax.random.permutation(jax.random.fold_in(keys[1], 3), NBLK // BLK_DEV)
    left_sector = jax.vmap(lambda own, number: deal_out(jax.random.fold_in(keys[1], 2), own, number, BLK_DEV, N_SECTOR, 1, CAP, 2))(left_sector_keys, left_sector_turns).reshape((NBLK, 1))
    right_sector = set_ends(jax.random.randint(keys[2], (NBLK,), 0, RSEC), jax.random.fold_in(keys[2], 1), 0, RSEC - 1).astype(jnp.int32)
    left_blocks = noise(keys[3], (TERMS, N_SECTOR, BLOCK, BLOCK), BLOCK ** -0.5, 0.5, ((0, 8), (1, 4)))
    right_blocks = noise(keys[4], (TERMS, RSEC, BLOCK, BLOCK), (BLOCK * TERM_DEV * N_TERM) ** -0.5, 0.125, ((0, 8),))
    return {"wavefunction": wavefunction, "left_sector": left_sector, "right_sector": right_sector, "left_blocks": left_blocks, "right_blocks": right_blocks}


def reference(wavefunction, left_sector, right_sector, left_blocks, right_blocks):
    left_of = left_sector[:, 0].astype(jnp.int32)
    wave_wide = wavefunction.astype(jnp.float32)

    def add_term(summed, index_term):
        left_here = jnp.take(left_blocks[index_term], left_of, axis=0).astype(jnp.float32)
        mixed_left = jnp.einsum("kab,kbc->kac", left_here, wave_wide).astype(jnp.bfloat16)
        right_here = jnp.take(right_blocks[index_term], right_sector, axis=0).astype(jnp.float32)
        return summed + jnp.einsum("kac,kdc->kad", mixed_left.astype(jnp.float32), right_here), None

    summed, _ = lax.scan(add_term, jnp.zeros(wavefunction.shape, jnp.float32), jnp.arange(TERMS, dtype=jnp.int32))
    return summed.astype(jnp.bfloat16)
```

```python
import jax
import jax.numpy as jnp
from jax import lax
from jax.experimental import pallas as pl
from jax.experimental.pallas import tpu as pltpu
from jax.sharding import PartitionSpec as P


def product_kernel(ls_ref, rs_ref, wave_ref, left_ref, right_ref, out_ref):
    n_term, held = right_ref.shape[:2]
    order = wave_ref.shape[1]

    @pl.loop(0, wave_ref.shape[0])
    def _(k):
        left_at, right_at = ls_ref[k], rs_ref[k]
        wave = wave_ref[k]
        total = jnp.zeros((order, order), jnp.float32)
        for group in range(n_term):
            mixed = jnp.dot(
                left_ref[group, left_at], wave, preferred_element_type=jnp.float32
            ).astype(jnp.bfloat16)
            for t in range(held):
                total += lax.dot_general(
                    mixed[t * order : (t + 1) * order],
                    right_ref[group, t, right_at],
                    (((1,), (1,)), ((), ())),
                    preferred_element_type=jnp.float32,
                )
        out_ref[k] = total.astype(out_ref.dtype)


def local(wavefunction, left_sector, right_sector, left_blocks, right_blocks):
    n_sec = lax.axis_size("sector")
    n_term = lax.axis_size("term")
    order = wavefunction.shape[1]
    held, n_right = right_blocks.shape[:2]
    both = ("term", "sector")
    left_all = lax.all_gather(left_blocks.reshape(held * order, order), both, tiled=True)
    rows = held * n_right * order // n_sec
    share = lax.dynamic_slice_in_dim(
        right_blocks.reshape(-1, order), lax.axis_index("sector") * rows, rows
    )
    right_all = lax.all_gather(share, both, tiled=True)
    left_all = left_all.reshape(n_term, n_sec, held * order, order)
    right_all = right_all.reshape(n_term, held, n_right, order, order)
    nbytes = 2 * (wavefunction.size * 2 + left_all.size + right_all.size)
    smem = pl.BlockSpec(memory_space=pltpu.SMEM)
    vmem = pl.BlockSpec(memory_space=pltpu.VMEM)
    return pl.pallas_call(
        product_kernel,
        out_shape=jax.ShapeDtypeStruct(wavefunction.shape, wavefunction.dtype),
        in_specs=[smem, smem, vmem, vmem, vmem],
        out_specs=vmem,
        compiler_params=pltpu.CompilerParams(vmem_limit_bytes=nbytes + (8 << 20)),
        cost_estimate=pl.CostEstimate(
            flops=4 * wavefunction.size * order * held * n_term,
            bytes_accessed=nbytes,
            transcendentals=0,
        ),
    )(left_sector[:, 0], right_sector, wavefunction, left_all, right_all)


def solution(mesh):
    placed = (
        P(("term", "sector"), None, None),
        P(("term", "sector"), None),
        P(("term", "sector")),
        P("term", "sector", None, None),
        P("term", None, None, None),
    )
    return jax.shard_map(
        local,
        mesh=mesh,
        in_specs=placed,
        out_specs=P(("term", "sector"), None, None),
        check_vma=False,
    )
```

```python
import jax
import jax.numpy as jnp
from jax import lax
from jax.experimental import pallas as pl
from jax.experimental.pallas import tpu as pltpu
from jax.sharding import PartitionSpec as P


def neighbour_ring(n):
    return list(range(0, n, 2)) + list(range(1, n, 2))[::-1]


def from_behind(block, ring, distance):
    n = len(ring)
    route = [(ring[(i - distance) % n], ring[i]) for i in range(n)]
    return lax.ppermute(block, "term", route)


def from_sibling(block):
    n = lax.axis_size("sector")
    return lax.ppermute(block, "sector", [(i, i ^ 1) for i in range(n)])


def apply_groups(parts, groups, n_left, n_right):
    order = parts[0][1].shape[1]
    half = groups[0][0].shape[0] // n_left
    n_parts, n_groups = len(parts), len(groups)
    fresh = parts[0][0] is None

    def kernel(*refs):
        refs = list(refs)
        out_refs = refs[-n_parts:]
        group_refs = refs[:n_groups * 2]
        rest = refs[n_groups * 2 : -n_parts]
        for p in range(n_parts):
            ls_ref, rs_ref, wave_ref = rest[3 * p : 3 * p + 3]
            total_ref = None if fresh else rest[3 * n_parts + p]
            out_ref = out_refs[p]

            @pl.loop(0, wave_ref.shape[0], unroll=2)
            def _(k, ls_ref=ls_ref, rs_ref=rs_ref, wave_ref=wave_ref, total_ref=total_ref, out_ref=out_ref):
                left_at, right_at = ls_ref[k], rs_ref[k]
                lefts, rights = [], []
                for g in range(n_groups):
                    for h in range(half):
                        lefts.append(group_refs[2 * g][left_at * half + h])
                        rights.append(group_refs[2 * g + 1][h * n_right + right_at])
                mixed = jnp.dot(
                    jnp.concatenate(lefts, axis=0), wave_ref[k], preferred_element_type=jnp.float32
                ).astype(jnp.bfloat16)
                wide = jnp.concatenate(
                    [mixed[i * order : (i + 1) * order] for i in range(len(lefts))], axis=1
                )
                added = jnp.dot(
                    wide, jnp.concatenate(rights, axis=0), preferred_element_type=jnp.float32
                )
                out_ref[k] = added if fresh else total_ref[k] + added

    smem = pl.BlockSpec(memory_space=pltpu.SMEM)
    vmem = pl.BlockSpec(memory_space=pltpu.VMEM)
    operands, specs = [], []
    for left, right in groups:
        operands += [left, right]
        specs += [vmem, vmem]
    for _, wave, ls, rs in parts:
        operands += [ls, rs, wave]
        specs += [smem, smem, vmem]
    aliases = {}
    if not fresh:
        for p, part in enumerate(parts):
            aliases[len(operands)] = p
            operands.append(part[0])
            specs.append(vmem)
    nbytes = sum(x.size * x.dtype.itemsize for x in operands)
    waves = sum(part[1].size for part in parts)
    return pl.pallas_call(
        kernel,
        out_shape=[jax.ShapeDtypeStruct(part[1].shape, jnp.float32) for part in parts],
        in_specs=specs,
        out_specs=[vmem] * n_parts,
        input_output_aliases=aliases,
        compiler_params=pltpu.CompilerParams(vmem_limit_bytes=nbytes + 4 * waves + (8 << 20)),
        cost_estimate=pl.CostEstimate(
            flops=4 * waves * order * half * n_groups,
            bytes_accessed=nbytes + 4 * waves,
            transcendentals=0,
        ),
    )(*operands)


def local(wavefunction, left_sector, right_sector, left_blocks, right_blocks):
    n_sec = lax.axis_size("sector")
    n_term = lax.axis_size("term")
    order = wavefunction.shape[1]
    held, n_right = right_blocks.shape[:2]
    half = held // 2
    ring = neighbour_ring(n_term)
    core = lax.axis_index("sector") % 2

    left_halves = left_blocks.reshape(2, half, order, order)
    left_mine = lax.all_to_all(
        jnp.tile(left_halves, (n_sec // 2, 1, 1, 1)), "sector", split_axis=0, concat_axis=0, tiled=True
    ).reshape(n_sec * half, order, order)
    named = jnp.stack([left_sector[:, 0], right_sector])
    sibling_named, sibling_wave = from_sibling(named), from_sibling(wavefunction)
    right_mine = jnp.swapaxes(
        lax.dynamic_slice_in_dim(right_blocks, core * half, half), 2, 3
    ).reshape(half * n_right, order, order)
    n_own = n_sec * half
    own = jnp.concatenate([left_mine, right_mine], axis=0)

    def split(buffer):
        return buffer[:n_own], buffer[n_own:]

    def add(totals, groups):
        parts = [
            (totals[0], wavefunction, named[0], named[1]),
            (totals[1], sibling_wave, sibling_named[0], sibling_named[1]),
        ]
        return apply_groups(parts, groups, n_sec, n_right)

    totals = (None, None)
    ready, up, down = [split(own)], own, own
    for turn in range(1, n_term // 2):
        up, down = from_behind(up, ring, 1), from_behind(down, ring, -1)
        totals = add(totals, ready)
        ready = [split(up), split(down)]
    far_left = from_behind(up[:n_own], ring, 1)
    far_right = from_behind(down[n_own:], ring, -1)
    totals = add(totals, ready)
    last = [(far_left, far_right)]
    (for_sibling,) = apply_groups(
        [(totals[1], sibling_wave, sibling_named[0], sibling_named[1])], last, n_sec, n_right
    )
    returned = from_sibling(for_sibling.astype(jnp.bfloat16))
    (kept,) = apply_groups([(totals[0], wavefunction, named[0], named[1])], last, n_sec, n_right)
    return (kept + returned.astype(jnp.float32)).astype(wavefunction.dtype)


def solution(mesh):
    placed = (
        P(("term", "sector"), None, None),
        P(("term", "sector"), None),
        P(("term", "sector")),
        P("term", "sector", None, None),
        P("term", None, None, None),
    )
    return jax.shard_map(
        local,
        mesh=mesh,
        in_specs=placed,
        out_specs=P(("term", "sector"), None, None),
        check_vma=False,
    )
```

```python
import math

import jax
import jax.numpy as jnp
from jax import lax
from jax.experimental import pallas as pl
from jax.experimental.pallas import tpu as pltpu
from jax.sharding import PartitionSpec as P


def neighbour_ring(n):
    return list(range(0, n, 2)) + list(range(1, n, 2))[::-1]


def from_behind(block, ring, distance):
    n = len(ring)
    route = [(ring[(i - distance) % n], ring[i]) for i in range(n)]
    return lax.ppermute(block, "term", route)


def from_sector(block, offset):
    n = lax.axis_size("sector")
    return lax.ppermute(block, "sector", [(i, i ^ offset) for i in range(n)])


def apply_groups(parts, groups, n_left, n_right, out_dtype=jnp.float32):
    held, order = parts[0][1].shape[:2]
    half = groups[0][0].shape[0] // n_left
    n_parts, n_groups = len(parts), len(groups)
    fresh = parts[0][0] is None
    together = math.gcd(held, 4)

    def kernel(*refs):
        out_refs = refs[-n_parts:]
        group_refs = refs[: n_groups * 2]
        rest = refs[n_groups * 2 : -n_parts]

        def work_on(ls_ref, rs_ref, wave_ref, total_ref, out_ref):
            @pl.loop(0, held // together)
            def _(step):
                blocks = [step * together + i for i in range(together)]
                mixed, rights = [], []
                for k in blocks:
                    left_at, right_at = ls_ref[k], rs_ref[k]
                    lefts = [
                        group_refs[2 * g][left_at * half + h] for g in range(n_groups) for h in range(half)
                    ]
                    rights.append([
                        group_refs[2 * g + 1][h * n_right + right_at] for g in range(n_groups) for h in range(half)
                    ])
                    mixed.append(
                        jnp.dot(
                            jnp.concatenate(lefts, axis=0), wave_ref[k], preferred_element_type=jnp.float32
                        ).astype(jnp.bfloat16)
                    )
                added = []
                for one, right in zip(mixed, rights):
                    wide = jnp.concatenate(
                        [one[i * order : (i + 1) * order] for i in range(len(right))], axis=1
                    )
                    added.append(
                        jnp.dot(wide, jnp.concatenate(right, axis=0), preferred_element_type=jnp.float32)
                    )
                if total_ref is not None:
                    added = [total_ref[k] + one for k, one in zip(blocks, added)]
                for k, one in zip(blocks, added):
                    out_ref[k] = one.astype(out_ref.dtype)

        for p in range(n_parts):
            work_on(*rest[3 * p : 3 * p + 3], None if fresh else rest[3 * n_parts + p], out_refs[p])

    smem = pl.BlockSpec(memory_space=pltpu.SMEM)
    vmem = pl.BlockSpec(memory_space=pltpu.VMEM)
    operands, specs = [], []
    for left, right in groups:
        operands += [left, right]
        specs += [vmem, vmem]
    for _, wave, ls, rs in parts:
        operands += [ls, rs, wave]
        specs += [smem, smem, vmem]
    aliases = {}
    if not fresh:
        for p, part in enumerate(parts):
            if out_dtype == jnp.float32:
                aliases[len(operands)] = p
            operands.append(part[0])
            specs.append(vmem)
    nbytes = sum(x.size * x.dtype.itemsize for x in operands)
    waves = sum(part[1].size for part in parts)
    return pl.pallas_call(
        kernel,
        out_shape=[jax.ShapeDtypeStruct(part[1].shape, out_dtype) for part in parts],
        in_specs=specs,
        out_specs=[vmem] * n_parts,
        input_output_aliases=aliases,
        compiler_params=pltpu.CompilerParams(vmem_limit_bytes=nbytes + 4 * waves + (8 << 20)),
        cost_estimate=pl.CostEstimate(
            flops=4 * waves * order * half * n_groups,
            bytes_accessed=nbytes + 4 * waves,
            transcendentals=0,
        ),
    )(*operands)


def local(wavefunction, left_sector, right_sector, left_blocks, right_blocks):
    n_sec = lax.axis_size("sector")
    n_term = lax.axis_size("term")
    order = wavefunction.shape[1]
    held, n_right = right_blocks.shape[:2]
    half = held // 2
    ring = neighbour_ring(n_term)
    sector = lax.axis_index("sector")
    core = sector % 2

    right = jnp.swapaxes(lax.dynamic_slice_in_dim(right_blocks, core * half, half), 2, 3)
    right = right.reshape(half * n_right, order, order)
    left_halves = [
        lax.dynamic_slice_in_dim(left_blocks[:, 0], (core ^ other) * half, half) for other in range(2)
    ]
    left = jnp.concatenate(
        [left_halves[0]]
        + [from_sector(left_halves[slot % 2], slot) for slot in range(1, n_sec)],
        axis=0,
    )
    named = jnp.stack([left_sector[:, 0], right_sector])
    sibling_named, sibling_wave = from_sector(named, 1), from_sector(wavefunction, 1)
    here = (wavefunction, named[0] ^ sector, named[1])
    there = (sibling_wave, sibling_named[0] ^ sector, sibling_named[1])

    def add(totals, groups):
        return apply_groups([(totals[0], *here), (totals[1], *there)], groups, n_sec, n_right)

    totals = (None, None)
    ready = [(left, right)]
    right_up, right_down, left_up, left_down = right, right, left, left
    for turn in range(1, n_term // 2):
        right_up, right_down = from_behind(right_up, ring, 1), from_behind(right_down, ring, -1)
        left_up, left_down = from_behind(left_up, ring, 1), from_behind(left_down, ring, -1)
        totals = add(totals, ready)
        ready = [(left_up, right_up), (left_down, right_down)]
    far = [(from_behind(left_up, ring, 1), from_behind(right_down, ring, -1))]
    totals = add(totals, ready)
    (for_sibling,) = apply_groups([(totals[1], *there)], far, n_sec, n_right, jnp.bfloat16)
    returned = from_sector(for_sibling, 1)
    (kept,) = apply_groups([(totals[0], *here)], far, n_sec, n_right)
    return (kept + returned.astype(jnp.float32)).astype(wavefunction.dtype)


def solution(mesh):
    placed = (
        P(("term", "sector"), None, None),
        P(("term", "sector"), None),
        P(("term", "sector")),
        P("term", "sector", None, None),
        P("term", None, None, None),
    )
    return jax.shard_map(
        local,
        mesh=mesh,
        in_specs=placed,
        out_specs=P(("term", "sector"), None, None),
        check_vma=False,
    )
```

```python
import math

import jax
import jax.numpy as jnp
from jax import lax
from jax.experimental import pallas as pl
from jax.experimental.pallas import tpu as pltpu
from jax.sharding import PartitionSpec as P


def neighbour_ring(n):
    return list(range(0, n, 2)) + list(range(1, n, 2))[::-1]


def from_behind(block, ring, distance):
    n = len(ring)
    route = [(ring[(i - distance) % n], ring[i]) for i in range(n)]
    return lax.ppermute(block, "term", route)


def from_sector(block, offset):
    n = lax.axis_size("sector")
    return lax.ppermute(block, "sector", [(i, i ^ offset) for i in range(n)])


def apply_groups(parts, groups, n_left, n_right, out_dtype=jnp.float32):
    held, order = parts[0][1].shape[:2]
    half = groups[0][0].shape[0] // n_left
    n_parts, n_groups = len(parts), len(groups)
    fresh = parts[0][0] is None
    together = math.gcd(held, 16)

    def kernel(*refs):
        out_refs = refs[-n_parts:]
        group_refs = refs[: n_groups * 2]
        rest = refs[n_groups * 2 : -n_parts]

        def work_on(ls_ref, rs_ref, wave_ref, total_ref, out_ref):
            @pl.loop(0, held // together)
            def _(step):
                blocks = [step * together + i for i in range(together)]
                mixed, rights = [], []
                for k in blocks:
                    left_at, right_at = ls_ref[k], rs_ref[k]
                    lefts = [
                        group_refs[2 * g][left_at * half + h] for g in range(n_groups) for h in range(half)
                    ]
                    rights.append([
                        group_refs[2 * g + 1][h * n_right + right_at] for g in range(n_groups) for h in range(half)
                    ])
                    mixed.append(
                        jnp.dot(
                            jnp.concatenate(lefts, axis=0), wave_ref[k], preferred_element_type=jnp.float32
                        ).astype(jnp.bfloat16)
                    )
                added = []
                for one, right in zip(mixed, rights):
                    wide = jnp.concatenate(
                        [one[i * order : (i + 1) * order] for i in range(len(right))], axis=1
                    )
                    added.append(
                        jnp.dot(wide, jnp.concatenate(right, axis=0), preferred_element_type=jnp.float32)
                    )
                if total_ref is not None:
                    added = [total_ref[k] + one for k, one in zip(blocks, added)]
                for k, one in zip(blocks, added):
                    out_ref[k] = one.astype(out_ref.dtype)

        for p in range(n_parts):
            work_on(*rest[3 * p : 3 * p + 3], None if fresh else rest[3 * n_parts + p], out_refs[p])

    smem = pl.BlockSpec(memory_space=pltpu.SMEM)
    vmem = pl.BlockSpec(memory_space=pltpu.VMEM)
    operands, specs = [], []
    for left, right in groups:
        operands += [left, right]
        specs += [vmem, vmem]
    for _, wave, ls, rs in parts:
        operands += [ls, rs, wave]
        specs += [smem, smem, vmem]
    aliases = {}
    if not fresh:
        for p, part in enumerate(parts):
            if out_dtype == jnp.float32:
                aliases[len(operands)] = p
            operands.append(part[0])
            specs.append(vmem)
    nbytes = sum(x.size * x.dtype.itemsize for x in operands)
    waves = sum(part[1].size for part in parts)
    return pl.pallas_call(
        kernel,
        out_shape=[jax.ShapeDtypeStruct(part[1].shape, out_dtype) for part in parts],
        in_specs=specs,
        out_specs=[vmem] * n_parts,
        input_output_aliases=aliases,
        compiler_params=pltpu.CompilerParams(vmem_limit_bytes=nbytes + 4 * waves + (8 << 20)),
        cost_estimate=pl.CostEstimate(
            flops=4 * waves * order * half * n_groups,
            bytes_accessed=nbytes + 4 * waves,
            transcendentals=0,
        ),
    )(*operands)


def local(wavefunction, left_sector, right_sector, left_blocks, right_blocks):
    n_sec = lax.axis_size("sector")
    n_term = lax.axis_size("term")
    order = wavefunction.shape[1]
    held, n_right = right_blocks.shape[:2]
    half = held // 2
    ring = neighbour_ring(n_term)
    sector = lax.axis_index("sector")
    core = sector % 2

    right = jnp.swapaxes(lax.dynamic_slice_in_dim(right_blocks, core * half, half), 2, 3)
    right = right.reshape(half * n_right, order, order)
    left_halves = [
        lax.dynamic_slice_in_dim(left_blocks[:, 0], (core ^ other) * half, half) for other in range(2)
    ]
    left = jnp.concatenate(
        [left_halves[0]]
        + [from_sector(left_halves[slot % 2], slot) for slot in range(1, n_sec)],
        axis=0,
    )
    named = jnp.stack([left_sector[:, 0], right_sector])
    sibling_named, sibling_wave = from_sector(named, 1), from_sector(wavefunction, 1)
    here = (wavefunction, named[0] ^ sector, named[1])
    there = (sibling_wave, sibling_named[0] ^ sector, sibling_named[1])

    def add(totals, groups):
        return apply_groups([(totals[0], *here), (totals[1], *there)], groups, n_sec, n_right)

    totals = (None, None)
    ready = [(left, right)]
    right_up, right_down, left_up, left_down = right, right, left, left
    for turn in range(1, n_term // 2):
        right_up, right_down = from_behind(right_up, ring, 1), from_behind(right_down, ring, -1)
        left_up, left_down = from_behind(left_up, ring, 1), from_behind(left_down, ring, -1)
        totals = add(totals, ready)
        ready = [(left_up, right_up), (left_down, right_down)]
        right_down, totals = lax.optimization_barrier((right_down, totals))
    far = [(from_behind(left_up, ring, 1), from_behind(right_down, ring, -1))]
    totals = add(totals, ready)
    (for_sibling,) = apply_groups([(totals[1], *there)], far, n_sec, n_right, jnp.bfloat16)
    returned = from_sector(for_sibling, 1)
    (kept,) = apply_groups([(totals[0], *here)], far, n_sec, n_right)
    return (kept + returned.astype(jnp.float32)).astype(wavefunction.dtype)


def solution(mesh):
    placed = (
        P(("term", "sector"), None, None),
        P(("term", "sector"), None),
        P(("term", "sector")),
        P("term", "sector", None, None),
        P("term", None, None, None),
    )
    return jax.shard_map(
        local,
        mesh=mesh,
        in_specs=placed,
        out_specs=P(("term", "sector"), None, None),
        check_vma=False,
    )
```

```python
import jax
import jax.numpy as jnp
from jax import lax
from jax.experimental import pallas as pl
from jax.experimental.pallas import tpu as pltpu
from jax.sharding import PartitionSpec as P


def neighbour_ring(n):
    return list(range(0, n, 2)) + list(range(1, n, 2))[::-1]


def from_behind(block, ring, distance):
    n = len(ring)
    route = [(ring[(i - distance) % n], ring[i]) for i in range(n)]
    return lax.ppermute(block, "term", route)


def from_sector(block, offset):
    n = lax.axis_size("sector")
    return lax.ppermute(block, "sector", [(i, i ^ offset) for i in range(n)])


def apply_groups(parts, table, groups, n_left, n_right, out_dtype=jnp.float32):
    held, order = parts[0][1].shape[:2]
    half = groups[0][0].shape[0] // n_left
    n_parts, n_groups = len(parts), len(groups)
    fresh = parts[0][0] is None
    terms = [(g, h) for g in range(n_groups) for h in range(half)]

    def kernel(*refs):
        table_ref, refs = refs[0], refs[1:]
        group_refs = refs[: n_groups * 2]
        wave_refs = refs[n_groups * 2 : n_groups * 2 + n_parts]
        total_refs = refs[n_groups * 2 + n_parts : -n_parts]
        out_refs = refs[-n_parts:]

        def mix(p, k):
            at = table_ref[parts[p][2], k]
            lefts = [group_refs[2 * g][at * half + h] for g, h in terms]
            return jnp.dot(
                jnp.concatenate(lefts, axis=0), wave_refs[p][k], preferred_element_type=jnp.float32
            )

        def finish(p, k, mixed):
            at = table_ref[parts[p][2] + 1, k]
            rights = [group_refs[2 * g + 1][h * n_right + at] for g, h in terms]
            mixed = mixed.astype(jnp.bfloat16)
            wide = jnp.concatenate(
                [mixed[i * order : (i + 1) * order] for i in range(len(terms))], axis=1
            )
            return jnp.dot(wide, jnp.concatenate(rights, axis=0), preferred_element_type=jnp.float32)

        def store(p, k, added):
            total = added if fresh else total_refs[p][k] + added
            out_refs[p][k] = total.astype(out_dtype)

        work = [(p, k) for p in range(n_parts) for k in range(held)]
        apart = 3
        mixed, added = {}, {}
        for i in range(len(work) + 2 * apart):
            if i < len(work):
                mixed[i] = mix(*work[i])
            if 0 <= i - apart < len(work):
                added[i - apart] = finish(*work[i - apart], mixed.pop(i - apart))
            if 0 <= i - 2 * apart < len(work):
                store(*work[i - 2 * apart], added.pop(i - 2 * apart))

    smem = pl.BlockSpec(memory_space=pltpu.SMEM)
    vmem = pl.BlockSpec(memory_space=pltpu.VMEM)
    operands = [table] + [x for group in groups for x in group] + [part[1] for part in parts]
    aliases = {}
    if not fresh:
        if out_dtype == jnp.float32:
            aliases = {len(operands) + p: p for p in range(n_parts)}
        operands += [part[0] for part in parts]
    nbytes = sum(x.size * x.dtype.itemsize for x in operands)
    waves = sum(part[1].size for part in parts)
    return pl.pallas_call(
        kernel,
        out_shape=[jax.ShapeDtypeStruct(part[1].shape, out_dtype) for part in parts],
        in_specs=[smem] + [vmem] * (len(operands) - 1),
        out_specs=[vmem] * n_parts,
        input_output_aliases=aliases,
        compiler_params=pltpu.CompilerParams(vmem_limit_bytes=nbytes + 4 * waves + (8 << 20)),
        cost_estimate=pl.CostEstimate(
            flops=4 * waves * order * len(terms),
            bytes_accessed=nbytes + 4 * waves,
            transcendentals=0,
        ),
    )(*operands)


def local(wavefunction, left_sector, right_sector, left_blocks, right_blocks):
    n_sec = lax.axis_size("sector")
    n_term = lax.axis_size("term")
    order = wavefunction.shape[1]
    held, n_right = right_blocks.shape[:2]
    half = held // 2
    ring = neighbour_ring(n_term)
    sector = lax.axis_index("sector")
    core = sector % 2

    right = jnp.swapaxes(lax.dynamic_slice_in_dim(right_blocks, core * half, half), 2, 3)
    right = right.reshape(half * n_right, order, order)
    left_halves = [
        lax.dynamic_slice_in_dim(left_blocks[:, 0], (core ^ other) * half, half) for other in range(2)
    ]
    left = jnp.concatenate(
        [left_halves[0]]
        + [from_sector(left_halves[slot % 2], slot) for slot in range(1, n_sec)],
        axis=0,
    )
    named = jnp.stack([left_sector[:, 0], right_sector])
    sibling_named, sibling_wave = from_sector(named, 1), from_sector(wavefunction, 1)
    table = jnp.stack([named[0] ^ sector, named[1], sibling_named[0] ^ sector, sibling_named[1]])

    def add(totals, groups):
        parts = [(totals[0], wavefunction, 0), (totals[1], sibling_wave, 2)]
        return apply_groups(parts, table, groups, n_sec, n_right)

    totals = (None, None)
    ready = [(left, right)]
    right_up, right_down, left_up, left_down = right, right, left, left
    for turn in range(1, n_term // 2):
        right_up, right_down = from_behind(right_up, ring, 1), from_behind(right_down, ring, -1)
        left_up, left_down = from_behind(left_up, ring, 1), from_behind(left_down, ring, -1)
        totals = add(totals, ready)
        ready = [(left_up, right_up), (left_down, right_down)]
        right_down, totals = lax.optimization_barrier((right_down, totals))
    far = [(from_behind(left_up, ring, 1), from_behind(right_down, ring, -1))]
    totals = add(totals, ready)
    (for_sibling,) = apply_groups(
        [(totals[1], sibling_wave, 2)], table, far, n_sec, n_right, jnp.bfloat16
    )
    returned = from_sector(for_sibling, 1)
    (kept,) = apply_groups([(totals[0], wavefunction, 0)], table, far, n_sec, n_right)
    return (kept + returned.astype(jnp.float32)).astype(wavefunction.dtype)


def solution(mesh):
    placed = (
        P(("term", "sector"), None, None),
        P(("term", "sector"), None),
        P(("term", "sector")),
        P("term", "sector", None, None),
        P("term", None, None, None),
    )
    return jax.shard_map(
        local,
        mesh=mesh,
        in_specs=placed,
        out_specs=P(("term", "sector"), None, None),
        check_vma=False,
    )
```

```python
import jax
import jax.numpy as jnp
from jax import lax
from jax.experimental import pallas as pl
from jax.experimental.pallas import tpu as pltpu
from jax.sharding import PartitionSpec as P


def neighbour_ring(n):
    return list(range(0, n, 2)) + list(range(1, n, 2))[::-1]


def from_behind(block, ring, distance):
    n = len(ring)
    route = [(ring[(i - distance) % n], ring[i]) for i in range(n)]
    return lax.ppermute(block, "term", route)


def from_sector(block, offset):
    n = lax.axis_size("sector")
    return lax.ppermute(block, "sector", [(i, i ^ offset) for i in range(n)])


def apply_groups(parts, table, groups, n_left, n_right, out_dtype=jnp.float32):
    held, order = parts[0][1].shape[:2]
    half = groups[0][0].shape[0] // n_left
    n_parts, n_groups = len(parts), len(groups)
    fresh = parts[0][0] is None
    terms = [(g, h) for g in range(n_groups) for h in range(half)]

    def kernel(*refs):
        table_ref, refs = refs[0], refs[1:]
        group_refs = refs[: n_groups * 2]
        wave_refs = refs[n_groups * 2 : n_groups * 2 + n_parts]
        total_refs = refs[n_groups * 2 + n_parts : -n_parts]
        out_refs = refs[-n_parts:]

        def mix(p, k):
            lefts = []
            for g, h in terms:
                pair = [group_refs[2 * g][table_ref[parts[p][2], k + i] * half + h] for i in range(2)]
                lefts.append(jnp.concatenate(pair, axis=1))
            zeros = jnp.zeros((order, order), wave_refs[p].dtype)
            diagonal = jnp.concatenate(
                [
                    jnp.concatenate([wave_refs[p][k], zeros], axis=1),
                    jnp.concatenate([zeros, wave_refs[p][k + 1]], axis=1),
                ],
                axis=0,
            )
            return jnp.dot(jnp.concatenate(lefts, axis=0), diagonal, preferred_element_type=jnp.float32)

        def finish(p, k, mixed):
            mixed = mixed.astype(jnp.bfloat16)
            added = []
            for i in range(2):
                at = table_ref[parts[p][2] + 1, k + i]
                rights = [group_refs[2 * g + 1][h * n_right + at] for g, h in terms]
                wide = jnp.concatenate(
                    [
                        mixed[j * order : (j + 1) * order, i * order : (i + 1) * order]
                        for j in range(len(terms))
                    ],
                    axis=1,
                )
                added.append(
                    jnp.dot(wide, jnp.concatenate(rights, axis=0), preferred_element_type=jnp.float32)
                )
            return added

        def store(p, k, added):
            for i in range(2):
                total = added[i] if fresh else total_refs[p][k + i] + added[i]
                out_refs[p][k + i] = total.astype(out_dtype)

        work = [(p, k) for p in range(n_parts) for k in range(0, held, 2)]
        apart = 2
        mixed, added = {}, {}
        for i in range(len(work) + 2 * apart):
            if i < len(work):
                mixed[i] = mix(*work[i])
            if 0 <= i - apart < len(work):
                added[i - apart] = finish(*work[i - apart], mixed.pop(i - apart))
            if 0 <= i - 2 * apart < len(work):
                store(*work[i - 2 * apart], added.pop(i - 2 * apart))

    smem = pl.BlockSpec(memory_space=pltpu.SMEM)
    vmem = pl.BlockSpec(memory_space=pltpu.VMEM)
    operands = [table] + [x for group in groups for x in group] + [part[1] for part in parts]
    aliases = {}
    if not fresh:
        if out_dtype == jnp.float32:
            aliases = {len(operands) + p: p for p in range(n_parts)}
        operands += [part[0] for part in parts]
    nbytes = sum(x.size * x.dtype.itemsize for x in operands)
    waves = sum(part[1].size for part in parts)
    return pl.pallas_call(
        kernel,
        out_shape=[jax.ShapeDtypeStruct(part[1].shape, out_dtype) for part in parts],
        in_specs=[smem] + [vmem] * (len(operands) - 1),
        out_specs=[vmem] * n_parts,
        input_output_aliases=aliases,
        compiler_params=pltpu.CompilerParams(vmem_limit_bytes=nbytes + 4 * waves + (8 << 20)),
        cost_estimate=pl.CostEstimate(
            flops=4 * waves * order * len(terms),
            bytes_accessed=nbytes + 4 * waves,
            transcendentals=0,
        ),
    )(*operands)


def local(wavefunction, left_sector, right_sector, left_blocks, right_blocks):
    n_sec = lax.axis_size("sector")
    n_term = lax.axis_size("term")
    order = wavefunction.shape[1]
    held, n_right = right_blocks.shape[:2]
    half = held // 2
    ring = neighbour_ring(n_term)
    sector = lax.axis_index("sector")
    core = sector % 2

    right = jnp.swapaxes(lax.dynamic_slice_in_dim(right_blocks, core * half, half), 2, 3)
    right = right.reshape(half * n_right, order, order)
    right, left_blocks = lax.optimization_barrier((right, left_blocks))
    left_halves = [
        lax.dynamic_slice_in_dim(left_blocks[:, 0], (core ^ other) * half, half) for other in range(2)
    ]
    left = jnp.concatenate(
        [left_halves[0]]
        + [from_sector(left_halves[slot % 2], slot) for slot in range(1, n_sec)],
        axis=0,
    )
    named = jnp.stack([left_sector[:, 0], right_sector])
    sibling_named, sibling_wave = from_sector(named, 1), from_sector(wavefunction, 1)
    table = jnp.stack([named[0] ^ sector, named[1], sibling_named[0] ^ sector, sibling_named[1]])

    def add(totals, groups):
        parts = [(totals[0], wavefunction, 0), (totals[1], sibling_wave, 2)]
        return apply_groups(parts, table, groups, n_sec, n_right)

    totals = (None, None)
    ready = [(left, right)]
    right_up, right_down, left_up, left_down = right, right, left, left
    for turn in range(1, n_term // 2):
        right_up, right_down = from_behind(right_up, ring, 1), from_behind(right_down, ring, -1)
        left_up, left_down = from_behind(left_up, ring, 1), from_behind(left_down, ring, -1)
        totals = add(totals, ready)
        ready = [(left_up, right_up), (left_down, right_down)]
        left_up, left_down, totals, _, _ = lax.optimization_barrier(
            (left_up, left_down, totals, right_up, right_down)
        )
    far = [(from_behind(left_up, ring, 1), from_behind(right_down, ring, -1))]
    totals = add(totals, ready)
    (for_sibling,) = apply_groups(
        [(totals[1], sibling_wave, 2)], table, far, n_sec, n_right, jnp.bfloat16
    )
    returned = from_sector(for_sibling, 1)
    (kept,) = apply_groups([(totals[0], wavefunction, 0)], table, far, n_sec, n_right)
    return (kept + returned.astype(jnp.float32)).astype(wavefunction.dtype)


def solution(mesh):
    placed = (
        P(("term", "sector"), None, None),
        P(("term", "sector"), None),
        P(("term", "sector")),
        P("term", "sector", None, None),
        P("term", None, None, None),
    )
    return jax.shard_map(
        local,
        mesh=mesh,
        in_specs=placed,
        out_specs=P(("term", "sector"), None, None),
        check_vma=False,
    )
```

```python
import jax
import jax.numpy as jnp
from jax import lax
from jax.experimental import pallas as pl
from jax.experimental.pallas import tpu as pltpu
from jax.sharding import PartitionSpec as P


def neighbour_ring(n):
    return list(range(0, n, 2)) + list(range(1, n, 2))[::-1]


def from_behind(block, ring, distance):
    n = len(ring)
    route = [(ring[(i - distance) % n], ring[i]) for i in range(n)]
    return lax.ppermute(block, "term", route)


def from_sector(block, offset):
    n = lax.axis_size("sector")
    return lax.ppermute(block, "sector", [(i, i ^ offset) for i in range(n)])


def apply_groups(parts, table, groups, n_left, n_right, out_dtype=jnp.float32):
    held, order = parts[0][1].shape[:2]
    half = groups[0][0].shape[0] // n_left
    n_parts, n_groups = len(parts), len(groups)
    fresh = parts[0][0] is None
    terms = [(g, h) for g in range(n_groups) for h in range(half)]

    def kernel(*refs):
        table_ref, refs = refs[0], refs[1:]
        group_refs = refs[: n_groups * 2]
        wave_refs = refs[n_groups * 2 : n_groups * 2 + n_parts]
        total_refs = refs[n_groups * 2 + n_parts : -n_parts]
        out_refs = refs[-n_parts:]

        def mix(p, k):
            lefts = []
            for g, h in terms:
                pair = [group_refs[2 * g][table_ref[parts[p][2], k + i] * half + h] for i in range(2)]
                lefts.append(jnp.concatenate(pair, axis=1))
            zeros = jnp.zeros((order, order), wave_refs[p].dtype)
            diagonal = jnp.concatenate(
                [
                    jnp.concatenate([wave_refs[p][k], zeros], axis=1),
                    jnp.concatenate([zeros, wave_refs[p][k + 1]], axis=1),
                ],
                axis=0,
            )
            return jnp.dot(jnp.concatenate(lefts, axis=0), diagonal, preferred_element_type=jnp.float32)

        def finish(p, k, mixed):
            mixed = mixed.astype(jnp.bfloat16)
            at = [table_ref[parts[p][2] + 1, k + i] for i in range(2)]
            rights = [
                jnp.concatenate([group_refs[2 * g + 1][h * n_right + at[i]] for i in range(2)], axis=1)
                for g, h in terms
            ]
            wide = [
                jnp.concatenate(
                    [
                        mixed[j * order : (j + 1) * order, i * order : (i + 1) * order]
                        for j in range(len(terms))
                    ],
                    axis=1,
                )
                for i in range(2)
            ]
            both = jnp.dot(
                jnp.concatenate(wide, axis=0),
                jnp.concatenate(rights, axis=0),
                preferred_element_type=jnp.float32,
            )
            return [both[i * order : (i + 1) * order, i * order : (i + 1) * order] for i in range(2)]

        def store(p, k, added):
            for i in range(2):
                total = added[i] if fresh else total_refs[p][k + i] + added[i]
                out_refs[p][k + i] = total.astype(out_dtype)

        work = [(p, k) for p in range(n_parts) for k in range(0, held, 2)]
        apart = 2
        mixed, added = {}, {}
        for i in range(len(work) + 2 * apart):
            if i < len(work):
                mixed[i] = mix(*work[i])
            if 0 <= i - apart < len(work):
                added[i - apart] = finish(*work[i - apart], mixed.pop(i - apart))
            if 0 <= i - 2 * apart < len(work):
                store(*work[i - 2 * apart], added.pop(i - 2 * apart))

    smem = pl.BlockSpec(memory_space=pltpu.SMEM)
    vmem = pl.BlockSpec(memory_space=pltpu.VMEM)
    operands = [table] + [x for group in groups for x in group] + [part[1] for part in parts]
    aliases = {}
    if not fresh:
        if out_dtype == jnp.float32:
            aliases = {len(operands) + p: p for p in range(n_parts)}
        operands += [part[0] for part in parts]
    nbytes = sum(x.size * x.dtype.itemsize for x in operands)
    waves = sum(part[1].size for part in parts)
    return pl.pallas_call(
        kernel,
        out_shape=[jax.ShapeDtypeStruct(part[1].shape, out_dtype) for part in parts],
        in_specs=[smem] + [vmem] * (len(operands) - 1),
        out_specs=[vmem] * n_parts,
        input_output_aliases=aliases,
        compiler_params=pltpu.CompilerParams(vmem_limit_bytes=nbytes + 4 * waves + (8 << 20)),
        cost_estimate=pl.CostEstimate(
            flops=4 * waves * order * len(terms),
            bytes_accessed=nbytes + 4 * waves,
            transcendentals=0,
        ),
    )(*operands)


def local(wavefunction, left_sector, right_sector, left_blocks, right_blocks):
    n_sec = lax.axis_size("sector")
    n_term = lax.axis_size("term")
    order = wavefunction.shape[1]
    held, n_right = right_blocks.shape[:2]
    half = held // 2
    ring = neighbour_ring(n_term)
    sector = lax.axis_index("sector")
    core = sector % 2

    right = jnp.swapaxes(lax.dynamic_slice_in_dim(right_blocks, core * half, half), 2, 3)
    right = right.reshape(half * n_right, order, order)
    left_halves = [
        lax.dynamic_slice_in_dim(left_blocks[:, 0], (core ^ other) * half, half) for other in range(2)
    ]
    left = jnp.concatenate(
        [left_halves[0]]
        + [from_sector(left_halves[slot % 2], slot) for slot in range(1, n_sec)],
        axis=0,
    )
    named = jnp.stack([left_sector[:, 0], right_sector])
    sent_wave, _ = lax.optimization_barrier((wavefunction, left))
    sibling_named, sibling_wave = from_sector(named, 1), from_sector(sent_wave, 1)
    table = jnp.stack([named[0] ^ sector, named[1], sibling_named[0] ^ sector, sibling_named[1]])

    def add(totals, groups):
        parts = [(totals[0], wavefunction, 0), (totals[1], sibling_wave, 2)]
        return apply_groups(parts, table, groups, n_sec, n_right)

    totals = (None, None)
    ready = [(left, right)]
    right_up, right_down, left_up, left_down = right, right, left, left
    for turn in range(1, n_term // 2):
        right_up, right_down = from_behind(right_up, ring, 1), from_behind(right_down, ring, -1)
        left_up, left_down = from_behind(left_up, ring, 1), from_behind(left_down, ring, -1)
        totals = add(totals, ready)
        ready = [(left_up, right_up), (left_down, right_down)]
        left_up, left_down, totals, _, _ = lax.optimization_barrier(
            (left_up, left_down, totals, right_up, right_down)
        )
    far = [(from_behind(left_up, ring, 1), from_behind(right_down, ring, -1))]
    totals = add(totals, ready)
    (for_sibling,) = apply_groups(
        [(totals[1], sibling_wave, 2)], table, far, n_sec, n_right, jnp.bfloat16
    )
    returned = from_sector(for_sibling, 1)
    (kept,) = apply_groups([(totals[0], wavefunction, 0)], table, far, n_sec, n_right)
    return (kept + returned.astype(jnp.float32)).astype(wavefunction.dtype)


def solution(mesh):
    placed = (
        P(("term", "sector"), None, None),
        P(("term", "sector"), None),
        P(("term", "sector")),
        P("term", "sector", None, None),
        P("term", None, None, None),
    )
    return jax.shard_map(
        local,
        mesh=mesh,
        in_specs=placed,
        out_specs=P(("term", "sector"), None, None),
        check_vma=False,
    )
```

```python
import math

import jax
import jax.numpy as jnp
from jax import lax
from jax.experimental import pallas as pl
from jax.experimental.pallas import tpu as pltpu
from jax.sharding import PartitionSpec as P


def neighbour_ring(n):
    return list(range(0, n, 2)) + list(range(1, n, 2))[::-1]


def from_behind(block, ring, distance):
    n = len(ring)
    route = [(ring[(i - distance) % n], ring[i]) for i in range(n)]
    return lax.ppermute(block, "term", route)


def from_sector(block, offset):
    n = lax.axis_size("sector")
    return lax.ppermute(block, "sector", [(i, i ^ offset) for i in range(n)])


def apply_groups(parts, table, groups, n_left, n_right, out_dtype=jnp.float32):
    held, order = parts[0][1].shape[:2]
    half = groups[0][0].shape[0] // n_left
    n_parts, n_groups = len(parts), len(groups)
    fresh = parts[0][0] is None
    together = math.gcd(held, 16)
    terms = [(g, h) for g in range(n_groups) for h in range(half)]

    def kernel(*refs):
        table_ref, refs = refs[0], refs[1:]
        group_refs = refs[: n_groups * 2]
        wave_refs = refs[n_groups * 2 : n_groups * 2 + n_parts]
        total_refs = refs[n_groups * 2 + n_parts : -n_parts]
        out_refs = refs[-n_parts:]

        def work_on(p, first):
            blocks = [first + i for i in range(together)]
            mixed = []
            for k in blocks:
                at = table_ref[parts[p][2], k]
                lefts = [group_refs[2 * g][at * half + h] for g, h in terms]
                mixed.append(
                    jnp.dot(
                        jnp.concatenate(lefts, axis=0), wave_refs[p][k], preferred_element_type=jnp.float32
                    ).astype(jnp.bfloat16)
                )
            added = []
            for k, one in zip(blocks, mixed):
                at = table_ref[parts[p][2] + 1, k]
                rights = [group_refs[2 * g + 1][h * n_right + at] for g, h in terms]
                wide = jnp.concatenate(
                    [one[i * order : (i + 1) * order] for i in range(len(terms))], axis=1
                )
                added.append(
                    jnp.dot(wide, jnp.concatenate(rights, axis=0), preferred_element_type=jnp.float32)
                )
            for k, one in zip(blocks, added):
                total = one if fresh else total_refs[p][k] + one
                out_refs[p][k] = total.astype(out_dtype)

        for p in range(n_parts):
            for first in range(0, held, together):
                work_on(p, first)

    smem = pl.BlockSpec(memory_space=pltpu.SMEM)
    vmem = pl.BlockSpec(memory_space=pltpu.VMEM)
    operands = [table] + [x for group in groups for x in group] + [part[1] for part in parts]
    aliases = {}
    if not fresh:
        if out_dtype == jnp.float32:
            aliases = {len(operands) + p: p for p in range(n_parts)}
        operands += [part[0] for part in parts]
    nbytes = sum(x.size * x.dtype.itemsize for x in operands)
    waves = sum(part[1].size for part in parts)
    return pl.pallas_call(
        kernel,
        out_shape=[jax.ShapeDtypeStruct(part[1].shape, out_dtype) for part in parts],
        in_specs=[smem] + [vmem] * (len(operands) - 1),
        out_specs=[vmem] * n_parts,
        input_output_aliases=aliases,
        compiler_params=pltpu.CompilerParams(vmem_limit_bytes=nbytes + 4 * waves + (8 << 20)),
        cost_estimate=pl.CostEstimate(
            flops=4 * waves * order * len(terms),
            bytes_accessed=nbytes + 4 * waves,
            transcendentals=0,
        ),
    )(*operands)


def local(wavefunction, left_sector, right_sector, left_blocks, right_blocks):
    n_sec = lax.axis_size("sector")
    n_term = lax.axis_size("term")
    order = wavefunction.shape[1]
    held, n_right = right_blocks.shape[:2]
    half = held // 2
    ring = neighbour_ring(n_term)
    sector = lax.axis_index("sector")
    core = sector % 2

    right = jnp.swapaxes(lax.dynamic_slice_in_dim(right_blocks, core * half, half), 2, 3)
    right = right.reshape(half * n_right, order, order)
    left_halves = [
        lax.dynamic_slice_in_dim(left_blocks[:, 0], (core ^ other) * half, half) for other in range(2)
    ]
    left = jnp.concatenate(
        [left_halves[0]]
        + [from_sector(left_halves[slot % 2], slot) for slot in range(1, n_sec)],
        axis=0,
    )
    named = jnp.stack([left_sector[:, 0], right_sector])

    def add(totals, groups):
        parts = [(totals[0], wavefunction, 0), (totals[1], sibling_wave, 2)]
        return apply_groups(parts, table, groups, n_sec, n_right)

    totals, waiting = (None, None), [(left, right)]
    right_up, right_down, left_up, left_down = right, right, left, left
    for turn in range(1, n_term // 2):
        right_up, right_down = from_behind(right_up, ring, 1), from_behind(right_down, ring, -1)
        left_up, left_down = from_behind(left_up, ring, 1), from_behind(left_down, ring, -1)
        if turn == 1:
            sent_named, sent_wave, _ = lax.optimization_barrier((named, wavefunction, right_up))
            sibling_named, sibling_wave = from_sector(sent_named, 1), from_sector(sent_wave, 1)
            table = jnp.stack([named[0] ^ sector, named[1], sibling_named[0] ^ sector, sibling_named[1]])
        arrived = [(left_up, right_up), (left_down, right_down)]
        if turn > 1 and turn % 2 == 1:
            totals, waiting = add(totals, waiting[:-2]), waiting[-2:]
        left_up, left_down, _, _, totals = lax.optimization_barrier(
            (left_up, left_down, right_up, right_down, totals)
        )
        waiting += arrived
    far = [(from_behind(left_up, ring, 1), from_behind(right_down, ring, -1))]
    totals = add(totals, waiting)
    (for_sibling,) = apply_groups(
        [(totals[1], sibling_wave, 2)], table, far, n_sec, n_right, jnp.bfloat16
    )
    returned = from_sector(for_sibling, 1)
    (kept,) = apply_groups([(totals[0], wavefunction, 0)], table, far, n_sec, n_right)
    return (kept + returned.astype(jnp.float32)).astype(wavefunction.dtype)


def solution(mesh):
    placed = (
        P(("term", "sector"), None, None),
        P(("term", "sector"), None),
        P(("term", "sector")),
        P("term", "sector", None, None),
        P("term", None, None, None),
    )
    return jax.shard_map(
        local,
        mesh=mesh,
        in_specs=placed,
        out_specs=P(("term", "sector"), None, None),
        check_vma=False,
    )
```

```python
import math

import jax
import jax.numpy as jnp
from jax import lax
from jax.experimental import pallas as pl
from jax.experimental.pallas import tpu as pltpu
from jax.sharding import PartitionSpec as P


def from_term(block, offset):
    n = lax.axis_size("term")
    return lax.ppermute(block, "term", [(i, i ^ offset) for i in range(n)])


def from_sector(block, offset):
    n = lax.axis_size("sector")
    return lax.ppermute(block, "sector", [(i, i ^ offset) for i in range(n)])


def apply_groups(parts, table, groups, n_left, out_dtype=jnp.float32):
    held, order = parts[0][1].shape[:2]
    half = n_left // 2
    n_parts, n_groups, n_slots = len(parts), len(groups), len(groups[0])
    n_right = [message.shape[0] - n_left for message in groups[0]]
    step_right = n_right[0] // half
    fresh = parts[0][0] is None
    together = math.gcd(held, 16)
    terms = [(g, h) for g in range(n_groups) for h in range(half)]

    def kernel(*refs):
        table_ref, refs, (left_ref, right_ref) = refs[0], refs[1:-2], refs[-2:]
        group_refs = refs[: n_groups * n_slots]
        wave_refs = refs[n_groups * n_slots : n_groups * n_slots + n_parts]
        total_refs = refs[n_groups * n_slots + n_parts : -n_parts]
        out_refs = refs[-n_parts:]

        for g in range(n_groups):
            at_right = 0
            for slot in range(n_slots):
                message_ref = group_refs[g * n_slots + slot]
                left_ref[g, slot * n_left : (slot + 1) * n_left] = message_ref[:n_left]
                if n_right[slot]:
                    right_ref[g, at_right : at_right + n_right[slot]] = message_ref[n_left:]
                at_right += n_right[slot]

        def work_on(p, first):
            blocks = [first + i for i in range(together)]
            mixed = []
            for k in blocks:
                at = table_ref[parts[p][2], k]
                lefts = [left_ref[g, at * half + h] for g, h in terms]
                mixed.append(
                    jnp.dot(
                        jnp.concatenate(lefts, axis=0), wave_refs[p][k], preferred_element_type=jnp.float32
                    ).astype(jnp.bfloat16)
                )
            added = []
            for k, one in zip(blocks, mixed):
                at = table_ref[parts[p][2] + 1, k]
                rights = [right_ref[g, at + h * step_right] for g, h in terms]
                wide = jnp.concatenate(
                    [one[i * order : (i + 1) * order] for i in range(len(terms))], axis=1
                )
                added.append(
                    jnp.dot(wide, jnp.concatenate(rights, axis=0), preferred_element_type=jnp.float32)
                )
            for k, one in zip(blocks, added):
                total = one if fresh else total_refs[p][k] + one
                out_refs[p][k] = total.astype(out_dtype)

        for p in range(n_parts):
            for first in range(0, held, together):
                work_on(p, first)

    smem = pl.BlockSpec(memory_space=pltpu.SMEM)
    vmem = pl.BlockSpec(memory_space=pltpu.VMEM)
    operands = [table] + [x for group in groups for x in group] + [part[1] for part in parts]
    aliases = {}
    if not fresh:
        if out_dtype == jnp.float32:
            aliases = {len(operands) + p: p for p in range(n_parts)}
        operands += [part[0] for part in parts]
    scratch = [
        pltpu.VMEM((n_groups, n_slots * n_left, order, order), jnp.bfloat16),
        pltpu.VMEM((n_groups, sum(n_right), order, order), jnp.bfloat16),
    ]
    nbytes = sum(x.size * x.dtype.itemsize for x in operands)
    waves = sum(part[1].size for part in parts)
    return pl.pallas_call(
        kernel,
        out_shape=[jax.ShapeDtypeStruct(part[1].shape, out_dtype) for part in parts],
        in_specs=[smem] + [vmem] * (len(operands) - 1),
        out_specs=[vmem] * n_parts,
        scratch_shapes=scratch,
        input_output_aliases=aliases,
        compiler_params=pltpu.CompilerParams(vmem_limit_bytes=2 * nbytes + 4 * waves + (8 << 20)),
        cost_estimate=pl.CostEstimate(
            flops=4 * waves * order * len(terms),
            bytes_accessed=nbytes + 4 * waves,
            transcendentals=0,
        ),
    )(*operands)


def local(wavefunction, left_sector, right_sector, left_blocks, right_blocks):
    n_sec = lax.axis_size("sector")
    n_term = lax.axis_size("term")
    order = wavefunction.shape[1]
    held, n_right = right_blocks.shape[:2]
    half = held // 2
    sector = lax.axis_index("sector")
    core, chip = sector % 2, sector // 2
    n_chips = n_sec // 2
    shares = n_chips if n_right % n_chips == 0 else 1
    in_share = n_right // shares

    right = jnp.swapaxes(lax.dynamic_slice_in_dim(right_blocks, core * half, half), 2, 3)

    def right_share(slot):
        share = lax.dynamic_slice_in_dim(right, (chip ^ slot) % shares * in_share, in_share, axis=1)
        return share.reshape(half * in_share, order, order)

    left_halves = [
        lax.dynamic_slice_in_dim(left_blocks[:, 0], (core ^ other) * half, half) for other in range(2)
    ]
    left = jnp.concatenate([left_halves[0], from_sector(left_halves[1], 1)], axis=0)
    n_left = left.shape[0]
    own = [jnp.concatenate([left, right_share(0)], axis=0)]
    for slot in range(1, n_chips):
        other = from_sector(left, 2 * slot)
        own.append(jnp.concatenate([other, right_share(slot)], axis=0) if shares > 1 else other)

    def with_other_chips(message):
        passed = message if shares > 1 else message[:n_left]
        return [message] + [from_sector(passed, 2 * slot) for slot in range(1, n_chips)]

    groups = {0: own}
    first = {d: from_term(own[0], d) for d in range(4, n_term, 2)}
    for d in (1, 2):
        groups[d] = [from_term(message, d) for message in own]
    groups[3] = [from_term(message, 1) for message in groups[2]]
    for d in range(4, n_term, 2):
        groups[d] = with_other_chips(first[d])
        groups[d + 1] = with_other_chips(from_term(first[d], 1))

    named = jnp.stack([left_sector[:, 0], right_sector])
    sent_named, sent_wave, _ = lax.optimization_barrier((named, wavefunction, own[0]))
    sibling_named, sibling_wave = from_sector(sent_named, 1), from_sector(sent_wave, 1)
    rows = []
    for left_at, right_at in (named, sibling_named):
        share = (right_at // in_share) ^ (chip % shares)
        rows += [left_at ^ sector, share * half * in_share + right_at % in_share]
    table = jnp.stack(rows)

    arrival = sorted(range(n_term), key=lambda d: d if d < 3 or d % 2 == 0 else d + 1.5)
    early, last = arrival[:-2], arrival[-2:]
    totals = (None, None)
    for at in range(0, len(early), 3):
        parts = [(totals[0], wavefunction, 0), (totals[1], sibling_wave, 2)]
        totals = apply_groups(parts, table, [groups[d] for d in early[at : at + 3]], n_left)
    far = [groups[d] for d in last]
    (for_sibling,) = apply_groups([(totals[1], sibling_wave, 2)], table, far, n_left, jnp.bfloat16)
    returned = from_sector(for_sibling, 1)
    (kept,) = apply_groups([(totals[0], wavefunction, 0)], table, far, n_left)
    return (kept + returned.astype(jnp.float32)).astype(wavefunction.dtype)


def solution(mesh):
    placed = (
        P(("term", "sector"), None, None),
        P(("term", "sector"), None),
        P(("term", "sector")),
        P("term", "sector", None, None),
        P("term", None, None, None),
    )
    return jax.shard_map(
        local,
        mesh=mesh,
        in_specs=placed,
        out_specs=P(("term", "sector"), None, None),
        check_vma=False,
    )
```

```python
import math

import jax
import jax.numpy as jnp
from jax import lax
from jax.experimental import pallas as pl
from jax.experimental.pallas import tpu as pltpu
from jax.sharding import PartitionSpec as P


def neighbour_ring(n):
    return list(range(0, n, 2)) + list(range(1, n, 2))[::-1]


def along_ring(block, ring):
    n, n_sec = len(ring), lax.axis_size("sector")
    route = []
    for at in range(n):
        for sector in range(n_sec):
            to = (at + (1 if sector % 2 == 0 else -1)) % n
            route.append((ring[at] * n_sec + sector, ring[to] * n_sec + sector))
    return lax.ppermute(block, ("term", "sector"), route)


def from_sector(block, offset):
    n = lax.axis_size("sector")
    return lax.ppermute(block, "sector", [(i, i ^ offset) for i in range(n)])


def apply_groups(parts, table, groups, n_left, n_right, out_dtype=jnp.float32):
    held, order = parts[0][1].shape[:2]
    n_parts, n_groups = len(parts), len(groups)
    fresh = parts[0][0] is None
    together = math.gcd(held, 16)
    terms = [(g, t) for g, group in enumerate(groups) for t in range(group[2])]

    def kernel(*refs):
        table_ref, refs = refs[0], refs[1:]
        group_refs = refs[: n_groups * 2]
        wave_refs = refs[n_groups * 2 : n_groups * 2 + n_parts]
        total_refs = refs[n_groups * 2 + n_parts : -n_parts]
        out_refs = refs[-n_parts:]

        def operator(side, n_slots, g, t, slot):
            ref = group_refs[2 * g + side]
            skip = table_ref[4, 0] if ref.shape[0] > groups[g][2] * n_slots else 0
            return ref[(skip + t) * n_slots + slot]

        def work_on(p, first):
            blocks = [first + i for i in range(together)]
            mixed = []
            for k in blocks:
                slot = table_ref[parts[p][2], k]
                lefts = [operator(0, n_left, g, t, slot) for g, t in terms]
                mixed.append(
                    jnp.dot(
                        jnp.concatenate(lefts, axis=0), wave_refs[p][k], preferred_element_type=jnp.float32
                    ).astype(jnp.bfloat16)
                )
            added = []
            for k, one in zip(blocks, mixed):
                slot = table_ref[parts[p][2] + 1, k]
                rights = [operator(1, n_right, g, t, slot) for g, t in terms]
                wide = jnp.concatenate(
                    [one[i * order : (i + 1) * order] for i in range(len(terms))], axis=1
                )
                added.append(
                    jnp.dot(wide, jnp.concatenate(rights, axis=0), preferred_element_type=jnp.float32)
                )
            for k, one in zip(blocks, added):
                total = one if fresh else total_refs[p][k] + one
                out_refs[p][k] = total.astype(out_dtype)

        for p in range(n_parts):
            for first in range(0, held, together):
                work_on(p, first)

    smem = pl.BlockSpec(memory_space=pltpu.SMEM)
    vmem = pl.BlockSpec(memory_space=pltpu.VMEM)
    operands = [table] + [x for group in groups for x in group[:2]] + [part[1] for part in parts]
    aliases = {}
    if not fresh:
        if out_dtype == jnp.float32:
            aliases = {len(operands) + p: p for p in range(n_parts)}
        operands += [part[0] for part in parts]
    nbytes = sum(x.size * x.dtype.itemsize for x in operands)
    waves = sum(part[1].size for part in parts)
    return pl.pallas_call(
        kernel,
        out_shape=[jax.ShapeDtypeStruct(part[1].shape, out_dtype) for part in parts],
        in_specs=[smem] + [vmem] * (len(operands) - 1),
        out_specs=[vmem] * n_parts,
        input_output_aliases=aliases,
        compiler_params=pltpu.CompilerParams(vmem_limit_bytes=nbytes + 4 * waves + (8 << 20)),
        cost_estimate=pl.CostEstimate(
            flops=4 * waves * order * len(terms),
            bytes_accessed=nbytes + 4 * waves,
            transcendentals=0,
        ),
    )(*operands)


def local(wavefunction, left_sector, right_sector, left_blocks, right_blocks):
    n_sec = lax.axis_size("sector")
    n_term = lax.axis_size("term")
    order = wavefunction.shape[1]
    held, n_right = right_blocks.shape[:2]
    half = held // 2
    ring = neighbour_ring(n_term)
    sector = lax.axis_index("sector")
    core = sector % 2

    right = jnp.swapaxes(right_blocks, 2, 3).reshape(held * n_right, order, order)
    left = jnp.concatenate(
        [left_blocks] + [from_sector(left_blocks, slot) for slot in range(1, n_sec)], axis=1
    ).reshape(held * n_sec, order, order)
    named = jnp.stack([left_sector[:, 0], right_sector])

    def my_half(blocks):
        n = blocks.shape[0] // 2
        return lax.dynamic_slice_in_dim(blocks, core * n, n)

    totals, waiting = (None, None), [(left, right, half)]
    right_now, left_now = right, left
    for turn in range(1, n_term // 2):
        right_now, left_now = along_ring(right_now, ring), along_ring(left_now, ring)
        if turn == 1:
            sent_named, sent_wave, _ = lax.optimization_barrier((named, wavefunction, right_now))
            sibling_named, sibling_wave = from_sector(sent_named, 1), from_sector(sent_wave, 1)
            table = jnp.stack([
                named[0] ^ sector,
                named[1],
                sibling_named[0] ^ sector,
                sibling_named[1],
                jnp.broadcast_to(core * half, named.shape[1:]),
            ])
        arrived = (left_now, right_now, held)
        if turn > 1 and turn % 2 == 1:
            parts = [(totals[0], wavefunction, 0), (totals[1], sibling_wave, 2)]
            totals = apply_groups(parts, table, waiting[:-1], n_sec, n_right)
            waiting = waiting[-1:]
        left_now, _, totals = lax.optimization_barrier((left_now, right_now, totals))
        waiting.append(arrived)
    far = [(along_ring(my_half(left_now), ring), along_ring(my_half(right_now), ring), half)]
    parts = [(totals[0], wavefunction, 0), (totals[1], sibling_wave, 2)]
    totals = apply_groups(parts, table, waiting, n_sec, n_right)
    (for_sibling,) = apply_groups(
        [(totals[1], sibling_wave, 2)], table, far, n_sec, n_right, jnp.bfloat16
    )
    returned = from_sector(for_sibling, 1)
    (kept,) = apply_groups([(totals[0], wavefunction, 0)], table, far, n_sec, n_right)
    return (kept + returned.astype(jnp.float32)).astype(wavefunction.dtype)


def solution(mesh):
    placed = (
        P(("term", "sector"), None, None),
        P(("term", "sector"), None),
        P(("term", "sector")),
        P("term", "sector", None, None),
        P("term", None, None, None),
    )
    return jax.shard_map(
        local,
        mesh=mesh,
        in_specs=placed,
        out_specs=P(("term", "sector"), None, None),
        check_vma=False,
    )
```

```python
import math

import jax
import jax.numpy as jnp
from jax import lax
from jax.experimental import pallas as pl
from jax.experimental.pallas import tpu as pltpu
from jax.sharding import PartitionSpec as P


def neighbour_ring(n):
    return list(range(0, n, 2)) + list(range(1, n, 2))[::-1]


def along_ring(block, ring):
    n, n_sec = len(ring), lax.axis_size("sector")
    route = []
    for at in range(n):
        for sector in range(n_sec):
            to = (at + (1 if sector % 2 == 0 else -1)) % n
            route.append((ring[at] * n_sec + sector, ring[to] * n_sec + sector))
    return lax.ppermute(block, ("term", "sector"), route)


def from_sector(block, offset):
    n = lax.axis_size("sector")
    return lax.ppermute(block, "sector", [(i, i ^ offset) for i in range(n)])


def apply_groups(parts, table, groups, n_right, out_dtype=jnp.float32):
    held, order = parts[0][1].shape[:2]
    n_parts, n_groups, n_chips = len(parts), len(groups), len(groups[0][0])
    fresh = parts[0][0] is None
    together = math.gcd(held, 16)
    terms = [(g, t) for g, group in enumerate(groups) for t in range(group[2])]

    def kernel(*refs):
        table_ref, left_ref, refs = refs[0], refs[-1], refs[1:-1]
        n_operators = n_groups * (n_chips + 1)
        group_refs = [refs[g * (n_chips + 1) : (g + 1) * (n_chips + 1)] for g in range(n_groups)]
        wave_refs = refs[n_operators : n_operators + n_parts]
        total_refs = refs[n_operators + n_parts : -n_parts]
        out_refs = refs[-n_parts:]

        def place(ref, n_slots, g, t):
            skip = table_ref[4, 0] if ref.shape[0] > groups[g][2] * n_slots else 0
            return (skip + t) * n_slots

        for at, (g, t) in enumerate(terms):
            for chip in range(n_chips):
                ref = group_refs[g][chip]
                left_ref[at, 2 * chip : 2 * chip + 2] = ref[pl.ds(place(ref, 2, g, t), 2)]

        def right_of(g, t, slot):
            ref = group_refs[g][n_chips]
            return ref[place(ref, n_right, g, t) + slot]

        def work_on(p, first):
            blocks = [first + i for i in range(together)]
            mixed = []
            for k in blocks:
                slot = table_ref[parts[p][2], k]
                lefts = [left_ref[at, slot] for at in range(len(terms))]
                mixed.append(
                    jnp.dot(
                        jnp.concatenate(lefts, axis=0), wave_refs[p][k], preferred_element_type=jnp.float32
                    ).astype(jnp.bfloat16)
                )
            added = []
            for k, one in zip(blocks, mixed):
                slot = table_ref[parts[p][2] + 1, k]
                rights = [right_of(g, t, slot) for g, t in terms]
                wide = jnp.concatenate(
                    [one[i * order : (i + 1) * order] for i in range(len(terms))], axis=1
                )
                added.append(
                    lax.dot_general(
                        wide,
                        jnp.concatenate(rights, axis=1),
                        (((1,), (1,)), ((), ())),
                        preferred_element_type=jnp.float32,
                    )
                )
            for k, one in zip(blocks, added):
                total = one if fresh else total_refs[p][k] + one
                out_refs[p][k] = total.astype(out_dtype)

        for p in range(n_parts):
            for first in range(0, held, together):
                work_on(p, first)

    smem = pl.BlockSpec(memory_space=pltpu.SMEM)
    vmem = pl.BlockSpec(memory_space=pltpu.VMEM)
    operands = [table] + [x for lefts, right, _ in groups for x in (*lefts, right)] + [part[1] for part in parts]
    aliases = {}
    if not fresh:
        if out_dtype == jnp.float32:
            aliases = {len(operands) + p: p for p in range(n_parts)}
        operands += [part[0] for part in parts]
    nbytes = sum(x.size * x.dtype.itemsize for x in operands)
    waves = sum(part[1].size for part in parts)
    return pl.pallas_call(
        kernel,
        out_shape=[jax.ShapeDtypeStruct(part[1].shape, out_dtype) for part in parts],
        in_specs=[smem] + [vmem] * (len(operands) - 1),
        out_specs=[vmem] * n_parts,
        scratch_shapes=[pltpu.VMEM((len(terms), 2 * n_chips, order, order), jnp.bfloat16)],
        input_output_aliases=aliases,
        compiler_params=pltpu.CompilerParams(vmem_limit_bytes=2 * nbytes + 4 * waves + (8 << 20)),
        cost_estimate=pl.CostEstimate(
            flops=4 * waves * order * len(terms),
            bytes_accessed=nbytes + 4 * waves,
            transcendentals=0,
        ),
    )(*operands)


def local(wavefunction, left_sector, right_sector, left_blocks, right_blocks):
    n_sec = lax.axis_size("sector")
    n_term = lax.axis_size("term")
    order = wavefunction.shape[1]
    held, n_right = right_blocks.shape[:2]
    half = held // 2
    ring = neighbour_ring(n_term)
    sector = lax.axis_index("sector")
    core = sector % 2

    right = right_blocks.reshape(held * n_right, order, order)
    left = jnp.concatenate([left_blocks, from_sector(left_blocks, 1)], axis=1)
    left = left.reshape(2 * held, order, order)

    def with_other_chips(blocks):
        return [blocks] + [from_sector(blocks, slot) for slot in range(2, n_sec, 2)]

    named = jnp.stack([left_sector[:, 0], right_sector])

    def my_half(blocks):
        n = blocks.shape[0] // 2
        return lax.dynamic_slice_in_dim(blocks, core * n, n)

    totals, waiting = (None, None), [(with_other_chips(left), right, half)]
    right_now, left_now = right, left
    for turn in range(1, n_term // 2):
        right_now, left_now = along_ring(right_now, ring), along_ring(left_now, ring)
        if turn == 1:
            sent_named, sent_wave, _ = lax.optimization_barrier((named, wavefunction, left_now))
            sibling_named, sibling_wave = from_sector(sent_named, 1), from_sector(sent_wave, 1)
            table = jnp.stack([
                named[0] ^ sector,
                named[1],
                sibling_named[0] ^ sector,
                sibling_named[1],
                jnp.broadcast_to(core * half, named.shape[1:]),
            ])
        arrived = (with_other_chips(left_now), right_now, held)
        if turn > 1 and turn % 2 == 1:
            parts = [(totals[0], wavefunction, 0), (totals[1], sibling_wave, 2)]
            totals = apply_groups(parts, table, waiting[:-1], n_right)
            waiting = waiting[-1:]
            right_now, totals = lax.optimization_barrier((right_now, totals))
        waiting.append(arrived)
    far = [(with_other_chips(along_ring(my_half(left_now), ring)), along_ring(my_half(right_now), ring), half)]
    parts = [(totals[0], wavefunction, 0), (totals[1], sibling_wave, 2)]
    totals = apply_groups(parts, table, waiting, n_right)
    (for_sibling,) = apply_groups(
        [(totals[1], sibling_wave, 2)], table, far, n_right, jnp.bfloat16
    )
    returned = from_sector(for_sibling, 1)
    (kept,) = apply_groups([(totals[0], wavefunction, 0)], table, far, n_right)
    return (kept + returned.astype(jnp.float32)).astype(wavefunction.dtype)


def solution(mesh):
    placed = (
        P(("term", "sector"), None, None),
        P(("term", "sector"), None),
        P(("term", "sector")),
        P("term", "sector", None, None),
        P("term", None, None, None),
    )
    return jax.shard_map(
        local,
        mesh=mesh,
        in_specs=placed,
        out_specs=P(("term", "sector"), None, None),
        check_vma=False,
    )
```

```python
import math

import jax
import jax.numpy as jnp
from jax import lax
from jax.experimental import pallas as pl
from jax.experimental.pallas import tpu as pltpu
from jax.sharding import PartitionSpec as P


def neighbour_ring(n):
    return list(range(0, n, 2)) + list(range(1, n, 2))[::-1]


def along_ring(block, ring):
    n, n_sec = len(ring), lax.axis_size("sector")
    route = []
    for at in range(n):
        for sector in range(n_sec):
            to = (at + (1 if sector % 2 == 0 else -1)) % n
            route.append((ring[at] * n_sec + sector, ring[to] * n_sec + sector))
    return lax.ppermute(block, ("term", "sector"), route)


def from_sector(block, offset):
    n = lax.axis_size("sector")
    return lax.ppermute(block, "sector", [(i, i ^ offset) for i in range(n)])


def joined(blocks, extra):
    blocks = [blocks] + extra
    held, _, order, _ = blocks[0].shape

    def kernel(*refs):
        for slot, ref in enumerate(refs[:-1]):
            refs[-1][:, slot] = ref[:, 0]

    vmem = pl.BlockSpec(memory_space=pltpu.VMEM)
    return pl.pallas_call(
        kernel,
        out_shape=jax.ShapeDtypeStruct((held, len(blocks), order, order), blocks[0].dtype),
        in_specs=[vmem] * len(blocks),
        out_specs=vmem,
    )(*blocks)


def apply_groups(parts, table, groups, n_left, n_right, out_dtype=jnp.float32):
    held, order = parts[0][1].shape[:2]
    n_parts, n_groups, n_addends = len(parts), len(groups), len(parts[0][0])
    together = math.gcd(held, 16)
    terms = [(g, t) for g, group in enumerate(groups) for t in range(group[2])]

    def kernel(*refs):
        table_ref, refs = refs[0], refs[1:]
        group_refs = refs[: n_groups * 2]
        wave_refs = refs[n_groups * 2 : n_groups * 2 + n_parts]
        addend_refs = refs[n_groups * 2 + n_parts : -n_parts]
        out_refs = refs[-n_parts:]

        def operator(side, n_slots, g, t, slot):
            ref = group_refs[2 * g + side]
            skip = table_ref[4, 0] if ref.shape[0] > groups[g][2] * n_slots else 0
            return ref[(skip + t) * n_slots + slot]

        def work_on(p, first):
            blocks = [first + i for i in range(together)]
            mixed = []
            for k in blocks:
                slot = table_ref[parts[p][2], k]
                lefts = [operator(0, n_left, g, t, slot) for g, t in terms]
                mixed.append(
                    jnp.dot(
                        jnp.concatenate(lefts, axis=0), wave_refs[p][k], preferred_element_type=jnp.float32
                    ).astype(jnp.bfloat16)
                )
            added = []
            for k, one in zip(blocks, mixed):
                slot = table_ref[parts[p][2] + 1, k]
                rights = [operator(1, n_right, g, t, slot) for g, t in terms]
                wide = jnp.concatenate(
                    [one[i * order : (i + 1) * order] for i in range(len(terms))], axis=1
                )
                added.append(
                    lax.dot_general(
                        wide,
                        jnp.concatenate(rights, axis=1),
                        (((1,), (1,)), ((), ())),
                        preferred_element_type=jnp.float32,
                    )
                )
            for k, total in zip(blocks, added):
                for ref in addend_refs[p * n_addends : (p + 1) * n_addends]:
                    total += ref[k].astype(jnp.float32)
                out_refs[p][k] = total.astype(out_dtype)

        for p in range(n_parts):
            for first in range(0, held, together):
                work_on(p, first)

    smem = pl.BlockSpec(memory_space=pltpu.SMEM)
    vmem = pl.BlockSpec(memory_space=pltpu.VMEM)
    operands = [table] + [x for group in groups for x in group[:2]] + [part[1] for part in parts]
    aliases = {}
    if n_addends and out_dtype == jnp.float32:
        aliases = {len(operands) + p * n_addends: p for p in range(n_parts)}
    operands += [x for part in parts for x in part[0]]
    nbytes = sum(x.size * x.dtype.itemsize for x in operands)
    waves = sum(part[1].size for part in parts)
    return pl.pallas_call(
        kernel,
        out_shape=[jax.ShapeDtypeStruct(part[1].shape, out_dtype) for part in parts],
        in_specs=[smem] + [vmem] * (len(operands) - 1),
        out_specs=[vmem] * n_parts,
        input_output_aliases=aliases,
        compiler_params=pltpu.CompilerParams(vmem_limit_bytes=nbytes + 4 * waves + (8 << 20)),
        cost_estimate=pl.CostEstimate(
            flops=4 * waves * order * len(terms),
            bytes_accessed=nbytes + 4 * waves,
            transcendentals=0,
        ),
    )(*operands)


def local(wavefunction, left_sector, right_sector, left_blocks, right_blocks):
    n_sec = lax.axis_size("sector")
    n_term = lax.axis_size("term")
    order = wavefunction.shape[1]
    held, n_right = right_blocks.shape[:2]
    half = held // 2
    ring = neighbour_ring(n_term)
    sector = lax.axis_index("sector")
    core = sector % 2

    others = [from_sector(left_blocks, slot) for slot in range(1, n_sec)]
    left = joined(left_blocks, others).reshape(held * n_sec, order, order)
    right, _ = lax.optimization_barrier((right_blocks, others[0]))
    right = right.reshape(held * n_right, order, order)
    named = jnp.stack([left_sector[:, 0], right_sector])

    def my_half(blocks):
        n = blocks.shape[0] // 2
        return lax.dynamic_slice_in_dim(blocks, core * n, n)

    mine, sibling = [], []
    waiting = [(left, right, half)]
    right_now, left_now = right, left
    for turn in range(1, n_term // 2):
        right_now, left_now = along_ring(right_now, ring), along_ring(left_now, ring)
        if turn == 1:
            sent_named, sent_wave, _ = lax.optimization_barrier((named, wavefunction, right_now))
            sibling_named, sibling_wave = from_sector(sent_named, 1), from_sector(sent_wave, 1)
            table = jnp.stack([
                named[0] ^ sector,
                named[1],
                sibling_named[0] ^ sector,
                sibling_named[1],
                jnp.broadcast_to(core * half, named.shape[1:]),
            ])
        arrived = (left_now, right_now, held)
        if turn > 1 and turn % 2 == 1:
            parts = [(mine, wavefunction, 0), (sibling, sibling_wave, 2)]
            mine, sibling = apply_groups(parts, table, waiting[:-1], n_sec, n_right)
            waiting = waiting[-1:]
            right_now, mine, sibling = lax.optimization_barrier((right_now, mine, sibling))
            mine, sibling = [mine], [sibling]
        waiting.append(arrived)
    far = [(along_ring(my_half(left_now), ring), along_ring(my_half(right_now), ring), half)]
    parts = [(mine, wavefunction, 0), (sibling, sibling_wave, 2)]
    mine, sibling = apply_groups(parts, table, waiting, n_sec, n_right)
    (for_sibling,) = apply_groups([([sibling], sibling_wave, 2)], table, far, n_sec, n_right, jnp.bfloat16)
    returned = from_sector(for_sibling, 1)
    (kept,) = apply_groups([([mine], wavefunction, 0)], table, far, n_sec, n_right)
    return (kept + returned.astype(jnp.float32)).astype(wavefunction.dtype)


def solution(mesh):
    placed = (
        P(("term", "sector"), None, None),
        P(("term", "sector"), None),
        P(("term", "sector")),
        P("term", "sector", None, None),
        P("term", None, None, None),
    )
    return jax.shard_map(
        local,
        mesh=mesh,
        in_specs=placed,
        out_specs=P(("term", "sector"), None, None),
        check_vma=False,
    )
```

```python
import math

import jax
import jax.numpy as jnp
from jax import lax
from jax.experimental import pallas as pl
from jax.experimental.pallas import tpu as pltpu
from jax.sharding import PartitionSpec as P


def neighbour_ring(n):
    return list(range(0, n, 2)) + list(range(1, n, 2))[::-1]


def along_ring(block, ring):
    n, n_sec = len(ring), lax.axis_size("sector")
    route = []
    for at in range(n):
        for sector in range(n_sec):
            to = (at + (1 if sector % 2 == 0 else -1)) % n
            route.append((ring[at] * n_sec + sector, ring[to] * n_sec + sector))
    return lax.ppermute(block, ("term", "sector"), route)


def from_sector(block, offset):
    n = lax.axis_size("sector")
    return lax.ppermute(block, "sector", [(i, i ^ offset) for i in range(n)])


def apply_groups(parts, table, groups, n_left, n_right, out_dtype=jnp.float32):
    held, order = parts[0][1].shape[:2]
    n_parts, n_groups = len(parts), len(groups)
    fresh = parts[0][0] is None
    together = math.gcd(held, 16)
    terms = [(g, t) for g, group in enumerate(groups) for t in range(group[2])]

    def kernel(*refs):
        table_ref, refs = refs[0], refs[1:]
        group_refs = refs[: n_groups * 2]
        wave_refs = refs[n_groups * 2 : n_groups * 2 + n_parts]
        total_refs = refs[n_groups * 2 + n_parts : -n_parts]
        out_refs = refs[-n_parts:]

        def operator(side, n_slots, g, t, slot):
            ref = group_refs[2 * g + side]
            skip = table_ref[4, 0] if ref.shape[0] > groups[g][2] * n_slots else 0
            return ref[(skip + t) * n_slots + slot]

        def work_on(p, first):
            blocks = [first + i for i in range(together)]
            mixed = []
            for k in blocks:
                slot = table_ref[parts[p][2], k]
                lefts = [operator(0, n_left, g, t, slot) for g, t in terms]
                mixed.append(
                    jnp.dot(
                        jnp.concatenate(lefts, axis=0), wave_refs[p][k], preferred_element_type=jnp.float32
                    ).astype(jnp.bfloat16)
                )
            added = []
            for k, one in zip(blocks, mixed):
                slot = table_ref[parts[p][2] + 1, k]
                rights = [operator(1, n_right, g, t, slot) for g, t in terms]
                wide = jnp.concatenate(
                    [one[i * order : (i + 1) * order] for i in range(len(terms))], axis=1
                )
                added.append(
                    jnp.dot(wide, jnp.concatenate(rights, axis=0), preferred_element_type=jnp.float32)
                )
            for k, one in zip(blocks, added):
                total = one if fresh else total_refs[p][k] + one
                out_refs[p][k] = total.astype(out_dtype)

        for p in range(n_parts):
            for first in range(0, held, together):
                work_on(p, first)

    smem = pl.BlockSpec(memory_space=pltpu.SMEM)
    vmem = pl.BlockSpec(memory_space=pltpu.VMEM)
    operands = [table] + [x for group in groups for x in group[:2]] + [part[1] for part in parts]
    aliases = {}
    if not fresh:
        if out_dtype == jnp.float32:
            aliases = {len(operands) + p: p for p in range(n_parts)}
        operands += [part[0] for part in parts]
    nbytes = sum(x.size * x.dtype.itemsize for x in operands)
    waves = sum(part[1].size for part in parts)
    return pl.pallas_call(
        kernel,
        out_shape=[jax.ShapeDtypeStruct(part[1].shape, out_dtype) for part in parts],
        in_specs=[smem] + [vmem] * (len(operands) - 1),
        out_specs=[vmem] * n_parts,
        input_output_aliases=aliases,
        compiler_params=pltpu.CompilerParams(vmem_limit_bytes=nbytes + 4 * waves + (8 << 20)),
        cost_estimate=pl.CostEstimate(
            flops=4 * waves * order * len(terms),
            bytes_accessed=nbytes + 4 * waves,
            transcendentals=0,
        ),
    )(*operands)


def local(wavefunction, left_sector, right_sector, left_blocks, right_blocks):
    n_sec = lax.axis_size("sector")
    n_term = lax.axis_size("term")
    order = wavefunction.shape[1]
    held, n_right = right_blocks.shape[:2]
    half = held // 2
    ring = neighbour_ring(n_term)
    sector = lax.axis_index("sector")
    core = sector % 2

    right = jnp.swapaxes(right_blocks, 2, 3).reshape(held * n_right, order, order)
    pair = jnp.concatenate([left_blocks, from_sector(left_blocks, 1)], axis=1)
    others = [from_sector(left_blocks, slot) for slot in range(2, n_sec)]
    pair = lax.optimization_barrier(pair)
    left = jnp.concatenate([pair] + others, axis=1).reshape(held * n_sec, order, order)
    named = jnp.stack([left_sector[:, 0], right_sector])

    def my_half(blocks):
        n = blocks.shape[0] // 2
        return lax.dynamic_slice_in_dim(blocks, core * n, n)

    totals, waiting = (None, None), [(left, right, half)]
    right_now, left_now = right, left
    for turn in range(1, n_term // 2):
        right_now, left_now = along_ring(right_now, ring), along_ring(left_now, ring)
        if turn == 1:
            sent_named, sent_wave, _ = lax.optimization_barrier((named, wavefunction, right_now))
            sibling_named, sibling_wave = from_sector(sent_named, 1), from_sector(sent_wave, 1)
            table = jnp.stack([
                named[0] ^ sector,
                named[1],
                sibling_named[0] ^ sector,
                sibling_named[1],
                jnp.broadcast_to(core * half, named.shape[1:]),
            ])
        arrived = (left_now, right_now, held)
        if turn > 1 and turn % 2 == 1:
            parts = [(totals[0], wavefunction, 0), (totals[1], sibling_wave, 2)]
            totals = apply_groups(parts, table, waiting[:-1], n_sec, n_right)
            waiting = waiting[-1:]
            right_now, totals = lax.optimization_barrier((right_now, totals))
        else:
            left_now, _ = lax.optimization_barrier((left_now, right_now))
        waiting.append(arrived)
    far = [(along_ring(my_half(left_now), ring), along_ring(my_half(right_now), ring), half)]
    parts = [(totals[0], wavefunction, 0), (totals[1], sibling_wave, 2)]
    totals = apply_groups(parts, table, waiting, n_sec, n_right)
    (for_sibling,) = apply_groups(
        [(totals[1], sibling_wave, 2)], table, far, n_sec, n_right, jnp.bfloat16
    )
    returned = from_sector(for_sibling, 1)
    (kept,) = apply_groups([(totals[0], wavefunction, 0)], table, far, n_sec, n_right)
    return (kept + returned.astype(jnp.float32)).astype(wavefunction.dtype)


def solution(mesh):
    placed = (
        P(("term", "sector"), None, None),
        P(("term", "sector"), None),
        P(("term", "sector")),
        P("term", "sector", None, None),
        P("term", None, None, None),
    )
    return jax.shard_map(
        local,
        mesh=mesh,
        in_specs=placed,
        out_specs=P(("term", "sector"), None, None),
        check_vma=False,
    )
```

```python
import math

import jax
import jax.numpy as jnp
from jax import lax
from jax.experimental import pallas as pl
from jax.experimental.pallas import tpu as pltpu
from jax.sharding import PartitionSpec as P


def neighbour_ring(n):
    return list(range(0, n, 2)) + list(range(1, n, 2))[::-1]


def along_ring(block, ring, cores=(0, 1)):
    n, n_sec = len(ring), lax.axis_size("sector")
    route = []
    for at in range(n):
        for sector in range(n_sec):
            if sector % 2 in cores:
                to = (at + (1 if sector % 2 == 0 else -1)) % n
                route.append((ring[at] * n_sec + sector, ring[to] * n_sec + sector))
    return lax.ppermute(block, ("term", "sector"), route)


def from_sector(block, offset):
    n = lax.axis_size("sector")
    return lax.ppermute(block, "sector", [(i, i ^ offset) for i in range(n)])


def apply_groups(parts, table, groups, n_left, n_right, out_dtype=jnp.float32):
    held, order = parts[0][1].shape[:2]
    n_parts, n_groups = len(parts), len(groups)
    fresh = parts[0][0] is None
    together = math.gcd(held, 16)
    terms = [(g, t) for g, group in enumerate(groups) for t in range(group[2])]

    def kernel(*refs):
        table_ref, refs = refs[0], refs[1:]
        group_refs = refs[: n_groups * 2]
        wave_refs = refs[n_groups * 2 : n_groups * 2 + n_parts]
        total_refs = refs[n_groups * 2 + n_parts : -n_parts]
        out_refs = refs[-n_parts:]

        def operator(side, n_slots, g, t, slot):
            ref = group_refs[2 * g + side]
            skip = table_ref[4, 0] if ref.shape[0] > groups[g][2] * n_slots else 0
            return ref[(skip + t) * n_slots + slot]

        def work_on(p, first):
            blocks = [first + i for i in range(together)]
            mixed = []
            for k in blocks:
                slot = table_ref[parts[p][2], k]
                lefts = [operator(0, n_left, g, t, slot) for g, t in terms]
                mixed.append(
                    jnp.dot(
                        jnp.concatenate(lefts, axis=0), wave_refs[p][k], preferred_element_type=jnp.float32
                    ).astype(jnp.bfloat16)
                )
            added = []
            for k, one in zip(blocks, mixed):
                slot = table_ref[parts[p][2] + 1, k]
                rights = [operator(1, n_right, g, t, slot) for g, t in terms]
                wide = jnp.concatenate(
                    [one[i * order : (i + 1) * order] for i in range(len(terms))], axis=1
                )
                added.append(
                    jnp.dot(wide, jnp.concatenate(rights, axis=0), preferred_element_type=jnp.float32)
                )
            for k, one in zip(blocks, added):
                total = one if fresh else total_refs[p][k] + one
                out_refs[p][k] = total.astype(out_dtype)

        for p in range(n_parts):
            for first in range(0, held, together):
                work_on(p, first)

    smem = pl.BlockSpec(memory_space=pltpu.SMEM)
    vmem = pl.BlockSpec(memory_space=pltpu.VMEM)
    operands = [table] + [x for group in groups for x in group[:2]] + [part[1] for part in parts]
    aliases = {}
    if not fresh:
        if out_dtype == jnp.float32:
            aliases = {len(operands) + p: p for p in range(n_parts)}
        operands += [part[0] for part in parts]
    nbytes = sum(x.size * x.dtype.itemsize for x in operands)
    waves = sum(part[1].size for part in parts)
    return pl.pallas_call(
        kernel,
        out_shape=[jax.ShapeDtypeStruct(part[1].shape, out_dtype) for part in parts],
        in_specs=[smem] + [vmem] * (len(operands) - 1),
        out_specs=[vmem] * n_parts,
        input_output_aliases=aliases,
        compiler_params=pltpu.CompilerParams(vmem_limit_bytes=nbytes + 4 * waves + (8 << 20)),
        cost_estimate=pl.CostEstimate(
            flops=4 * waves * order * len(terms),
            bytes_accessed=nbytes + 4 * waves,
            transcendentals=0,
        ),
    )(*operands)


def local(wavefunction, left_sector, right_sector, left_blocks, right_blocks):
    n_sec = lax.axis_size("sector")
    n_term = lax.axis_size("term")
    order = wavefunction.shape[1]
    held, n_right = right_blocks.shape[:2]
    half = held // 2
    ring = neighbour_ring(n_term)
    sector = lax.axis_index("sector")
    core = sector % 2

    right = jnp.swapaxes(right_blocks, 2, 3).reshape(held * n_right, order, order)
    pair = jnp.concatenate([left_blocks, from_sector(left_blocks, 1)], axis=1)
    others = [from_sector(left_blocks, slot) for slot in range(2, n_sec)]
    pair = lax.optimization_barrier(pair)
    left = jnp.concatenate([pair] + others, axis=1).reshape(held * n_sec, order, order)
    named = jnp.stack([left_sector[:, 0], right_sector])

    totals, waiting = (None, None), [(left, right, half)]
    right_now, left_now = right, left
    for turn in range(1, n_term // 2):
        right_now, left_now = along_ring(right_now, ring), along_ring(left_now, ring)
        if turn == 1:
            sent_named, sent_wave, _ = lax.optimization_barrier((named, wavefunction, right_now))
            sibling_named, sibling_wave = from_sector(sent_named, 1), from_sector(sent_wave, 1)
            table = jnp.stack([
                named[0] ^ sector,
                named[1],
                sibling_named[0] ^ sector,
                sibling_named[1],
                jnp.broadcast_to(core * half, named.shape[1:]),
            ])
        arrived = (left_now, right_now, held)
        if turn > 1 and turn % 2 == 1:
            parts = [(totals[0], wavefunction, 0), (totals[1], sibling_wave, 2)]
            totals = apply_groups(parts, table, waiting[:-1], n_sec, n_right)
            waiting = waiting[-1:]
            right_now, totals = lax.optimization_barrier((right_now, totals))
        else:
            left_now, _ = lax.optimization_barrier((left_now, right_now))
        waiting.append(arrived)
    far = [(along_ring(left_now, ring, (1,)), along_ring(right_now, ring, (1,)), held)]
    parts = [(totals[0], wavefunction, 0), (totals[1], sibling_wave, 2)]
    totals = apply_groups(parts, table, waiting, n_sec, n_right)
    (for_sibling,) = apply_groups(
        [(totals[1], sibling_wave, 2)], table, far, n_sec, n_right, jnp.bfloat16
    )
    returned = from_sector(for_sibling, 1)
    (kept,) = apply_groups([(totals[0], wavefunction, 0)], table, far, n_sec, n_right)
    return (kept + returned.astype(jnp.float32)).astype(wavefunction.dtype)


def solution(mesh):
    placed = (
        P(("term", "sector"), None, None),
        P(("term", "sector"), None),
        P(("term", "sector")),
        P("term", "sector", None, None),
        P("term", None, None, None),
    )
    return jax.shard_map(
        local,
        mesh=mesh,
        in_specs=placed,
        out_specs=P(("term", "sector"), None, None),
        check_vma=False,
    )
```

```python
import math

import jax
import jax.numpy as jnp
from jax import lax
from jax.experimental import pallas as pl
from jax.experimental.pallas import tpu as pltpu
from jax.sharding import PartitionSpec as P


def neighbour_ring(n):
    return list(range(0, n, 2)) + list(range(1, n, 2))[::-1]


def along_ring(block, ring):
    n, n_sec = len(ring), lax.axis_size("sector")
    route = []
    for at in range(n):
        for sector in range(n_sec):
            to = (at + (1 if sector % 2 == 0 else -1)) % n
            route.append((ring[at] * n_sec + sector, ring[to] * n_sec + sector))
    return lax.ppermute(block, ("term", "sector"), route)


def from_sector(block, offset):
    n = lax.axis_size("sector")
    return lax.ppermute(block, "sector", [(i, i ^ offset) for i in range(n)])


def apply_groups(parts, table, groups, n_left, n_right, out_dtype=jnp.float32):
    held, order = parts[0][1].shape[:2]
    n_parts, n_groups = len(parts), len(groups)
    fresh = parts[0][0] is None
    together = math.gcd(held, 16)
    terms = [(g, t) for g, group in enumerate(groups) for t in range(group[2])]

    def kernel(*refs):
        table_ref, refs = refs[0], refs[1:]
        group_refs = refs[: n_groups * 2]
        wave_refs = refs[n_groups * 2 : n_groups * 2 + n_parts]
        total_refs = refs[n_groups * 2 + n_parts : -n_parts]
        out_refs = refs[-n_parts:]

        def operator(side, n_slots, g, t, slot):
            ref = group_refs[2 * g + side]
            n_terms, other = groups[g][2:]
            skip = 0
            if ref.shape[0] > n_terms * n_slots:
                skip = n_terms - table_ref[4, 0] if other else table_ref[4, 0]
            return ref[(skip + t) * n_slots + slot]

        def work_on(p, first):
            blocks = [first + i for i in range(together)]
            mixed = []
            for k in blocks:
                slot = table_ref[parts[p][2], k]
                lefts = [operator(0, n_left, g, t, slot) for g, t in terms]
                mixed.append(
                    jnp.dot(
                        jnp.concatenate(lefts, axis=0), wave_refs[p][k], preferred_element_type=jnp.float32
                    ).astype(jnp.bfloat16)
                )
            added = []
            for k, one in zip(blocks, mixed):
                slot = table_ref[parts[p][2] + 1, k]
                rights = [operator(1, n_right, g, t, slot) for g, t in terms]
                wide = jnp.concatenate(
                    [one[i * order : (i + 1) * order] for i in range(len(terms))], axis=1
                )
                added.append(
                    jnp.dot(wide, jnp.concatenate(rights, axis=0), preferred_element_type=jnp.float32)
                )
            for k, one in zip(blocks, added):
                total = one if fresh else total_refs[p][k] + one
                out_refs[p][k] = total.astype(out_dtype)

        for p in range(n_parts):
            for first in range(0, held, together):
                work_on(p, first)

    smem = pl.BlockSpec(memory_space=pltpu.SMEM)
    vmem = pl.BlockSpec(memory_space=pltpu.VMEM)
    operands = [table] + [x for group in groups for x in group[:2]] + [part[1] for part in parts]
    aliases = {}
    if not fresh:
        if out_dtype == jnp.float32:
            aliases = {len(operands) + p: p for p in range(n_parts)}
        operands += [part[0] for part in parts]
    nbytes = sum(x.size * x.dtype.itemsize for x in operands)
    waves = sum(part[1].size for part in parts)
    return pl.pallas_call(
        kernel,
        out_shape=[jax.ShapeDtypeStruct(part[1].shape, out_dtype) for part in parts],
        in_specs=[smem] + [vmem] * (len(operands) - 1),
        out_specs=[vmem] * n_parts,
        input_output_aliases=aliases,
        compiler_params=pltpu.CompilerParams(vmem_limit_bytes=nbytes + 4 * waves + (8 << 20)),
        cost_estimate=pl.CostEstimate(
            flops=4 * waves * order * len(terms),
            bytes_accessed=nbytes + 4 * waves,
            transcendentals=0,
        ),
    )(*operands)


def local(wavefunction, left_sector, right_sector, left_blocks, right_blocks):
    n_sec = lax.axis_size("sector")
    n_term = lax.axis_size("term")
    order = wavefunction.shape[1]
    held, n_right = right_blocks.shape[:2]
    half = held // 2
    ring = neighbour_ring(n_term)
    sector = lax.axis_index("sector")
    core = sector % 2

    right = jnp.swapaxes(right_blocks, 2, 3).reshape(held * n_right, order, order)
    pair = jnp.concatenate([left_blocks, from_sector(left_blocks, 1)], axis=1)
    others = [from_sector(left_blocks, slot) for slot in range(2, n_sec)]
    pair = lax.optimization_barrier(pair)
    left = jnp.concatenate([pair] + others, axis=1).reshape(held * n_sec, order, order)
    named = jnp.stack([left_sector[:, 0], right_sector])

    def half_of(blocks, which):
        n = blocks.shape[0] // 2
        return lax.dynamic_slice_in_dim(blocks, which * n, n)

    totals, waiting = (None, None), [(left, right, half, False)]
    right_now, left_now = right, left
    for turn in range(1, n_term // 2):
        right_now = along_ring(right_now, ring)
        if turn < n_term // 2 - 1:
            left_now = along_ring(left_now, ring)
            arrived = [(left_now, right_now, held, False)]
        else:
            left_now, left_last = [along_ring(half_of(left_now, which), ring) for which in (core, 1 - core)]
            arrived = [(left_now, right_now, half, False), (left_last, right_now, half, True)]
        if turn == 1:
            sent_named, sent_wave, _ = lax.optimization_barrier((named, wavefunction, pair))
            sibling_named, sibling_wave = from_sector(sent_named, 1), from_sector(sent_wave, 1)
            table = jnp.stack([
                named[0] ^ sector,
                named[1],
                sibling_named[0] ^ sector,
                sibling_named[1],
                jnp.broadcast_to(core * half, named.shape[1:]),
            ])
        if turn % 2 == 0:
            parts = [(totals[0], wavefunction, 0), (totals[1], sibling_wave, 2)]
            totals = apply_groups(parts, table, waiting, n_sec, n_right)
            waiting = []
            left_now, totals = lax.optimization_barrier((left_now, totals))
        elif turn == 1:
            left_now, _ = lax.optimization_barrier((left_now, right_now))
        waiting += arrived
    far = [(along_ring(left_now, ring), along_ring(half_of(right_now, core), ring), half, False)]
    parts = [(totals[0], wavefunction, 0), (totals[1], sibling_wave, 2)]
    totals = apply_groups(parts, table, waiting, n_sec, n_right)
    (for_sibling,) = apply_groups(
        [(totals[1], sibling_wave, 2)], table, far, n_sec, n_right, jnp.bfloat16
    )
    returned = from_sector(for_sibling, 1)
    (kept,) = apply_groups([(totals[0], wavefunction, 0)], table, far, n_sec, n_right)
    return (kept + returned.astype(jnp.float32)).astype(wavefunction.dtype)


def solution(mesh):
    placed = (
        P(("term", "sector"), None, None),
        P(("term", "sector"), None),
        P(("term", "sector")),
        P("term", "sector", None, None),
        P("term", None, None, None),
    )
    return jax.shard_map(
        local,
        mesh=mesh,
        in_specs=placed,
        out_specs=P(("term", "sector"), None, None),
        check_vma=False,
    )
```

```python
import math

import jax
import jax.numpy as jnp
from jax import lax
from jax.experimental import pallas as pl
from jax.experimental.pallas import tpu as pltpu
from jax.sharding import PartitionSpec as P


def neighbour_ring(n):
    return list(range(0, n, 2)) + list(range(1, n, 2))[::-1]


def along_ring(block, ring):
    n, n_sec = len(ring), lax.axis_size("sector")
    route = []
    for at in range(n):
        for sector in range(n_sec):
            to = (at + (1 if sector % 2 == 0 else -1)) % n
            route.append((ring[at] * n_sec + sector, ring[to] * n_sec + sector))
    return lax.ppermute(block, ("term", "sector"), route)


def from_sector(block, offset):
    n = lax.axis_size("sector")
    return lax.ppermute(block, "sector", [(i, i ^ offset) for i in range(n)])


def apply_groups(parts, table, groups, n_left, n_right, out_dtype=jnp.float32):
    held, order = parts[0][1].shape[:2]
    n_parts, n_groups = len(parts), len(groups)
    fresh = parts[0][0] is None
    together = math.gcd(held, 16)
    terms = [(g, t) for g, group in enumerate(groups) for t in range(group[2])]

    def kernel(*refs):
        table_ref, refs = refs[0], refs[1:]
        group_refs = refs[: n_groups * 2]
        wave_refs = refs[n_groups * 2 : n_groups * 2 + n_parts]
        total_refs = refs[n_groups * 2 + n_parts : -n_parts]
        out_refs = refs[-n_parts:]

        def operator(side, n_slots, g, t, slot):
            ref = group_refs[2 * g + side]
            skip = table_ref[4, 0] if ref.shape[0] > groups[g][2] * n_slots else 0
            return ref[(skip + t) * n_slots + slot]

        def work_on(p, first):
            blocks = [first + i for i in range(together)]
            mixed = []
            for k in blocks:
                slot = table_ref[parts[p][2], k]
                lefts = [operator(0, n_left, g, t, slot) for g, t in terms]
                mixed.append(
                    jnp.dot(
                        jnp.concatenate(lefts, axis=0), wave_refs[p][k], preferred_element_type=jnp.float32
                    ).astype(jnp.bfloat16)
                )
            added = []
            for k, one in zip(blocks, mixed):
                slot = table_ref[parts[p][2] + 1, k]
                rights = [operator(1, n_right, g, t, slot) for g, t in terms]
                wide = jnp.concatenate(
                    [one[i * order : (i + 1) * order] for i in range(len(terms))], axis=1
                )
                added.append(
                    jnp.dot(wide, jnp.concatenate(rights, axis=0), preferred_element_type=jnp.float32)
                )
            for k, one in zip(blocks, added):
                total = one if fresh else total_refs[p][k] + one
                out_refs[p][k] = total.astype(out_dtype)

        for p in range(n_parts):
            for first in range(0, held, together):
                work_on(p, first)

    smem = pl.BlockSpec(memory_space=pltpu.SMEM)
    vmem = pl.BlockSpec(memory_space=pltpu.VMEM)
    operands = [table] + [x for group in groups for x in group[:2]] + [part[1] for part in parts]
    aliases = {}
    if not fresh:
        if out_dtype == jnp.float32:
            aliases = {len(operands) + p: p for p in range(n_parts)}
        operands += [part[0] for part in parts]
    nbytes = sum(x.size * x.dtype.itemsize for x in operands)
    waves = sum(part[1].size for part in parts)
    return pl.pallas_call(
        kernel,
        out_shape=[jax.ShapeDtypeStruct(part[1].shape, out_dtype) for part in parts],
        in_specs=[smem] + [vmem] * (len(operands) - 1),
        out_specs=[vmem] * n_parts,
        input_output_aliases=aliases,
        compiler_params=pltpu.CompilerParams(vmem_limit_bytes=nbytes + 4 * waves + (8 << 20)),
        cost_estimate=pl.CostEstimate(
            flops=4 * waves * order * len(terms),
            bytes_accessed=nbytes + 4 * waves,
            transcendentals=0,
        ),
    )(*operands)


def local(wavefunction, left_sector, right_sector, left_blocks, right_blocks):
    n_sec = lax.axis_size("sector")
    n_term = lax.axis_size("term")
    order = wavefunction.shape[1]
    held, n_right = right_blocks.shape[:2]
    half = held // 2
    ring = neighbour_ring(n_term)
    sector = lax.axis_index("sector")
    core = sector % 2

    right = jnp.swapaxes(right_blocks, 2, 3).reshape(held * n_right, order, order)
    far_slots = jnp.concatenate([from_sector(left_blocks, slot) for slot in range(2, n_sec)], axis=1)
    far_slots = lax.optimization_barrier(far_slots)
    room = ((0, 0), (0, n_sec - 1), (0, 0), (0, 0))
    laid_out = lax.optimization_barrier(jnp.pad(left_blocks, room))
    left = jnp.concatenate([laid_out[:, :1], from_sector(left_blocks, 1), far_slots], axis=1)
    left = left.reshape(held * n_sec, order, order)
    named = jnp.stack([left_sector[:, 0], right_sector])

    def my_half(blocks):
        n = blocks.shape[0] // 2
        return lax.dynamic_slice_in_dim(blocks, core * n, n)

    totals, waiting = (None, None), [(left, right, half)]
    right_now, left_now = right, left
    for turn in range(1, n_term // 2):
        right_now, left_now = along_ring(right_now, ring), along_ring(left_now, ring)
        if turn == 1:
            sent_named, sent_wave, _ = lax.optimization_barrier((named, wavefunction, right_now))
            sibling_named, sibling_wave = from_sector(sent_named, 1), from_sector(sent_wave, 1)
            table = jnp.stack([
                named[0] ^ sector,
                named[1],
                sibling_named[0] ^ sector,
                sibling_named[1],
                jnp.broadcast_to(core * half, named.shape[1:]),
            ])
        arrived = (left_now, right_now, held)
        if turn > 1 and turn % 2 == 1:
            parts = [(totals[0], wavefunction, 0), (totals[1], sibling_wave, 2)]
            totals = apply_groups(parts, table, waiting[:-1], n_sec, n_right)
            waiting = waiting[-1:]
            right_now, totals = lax.optimization_barrier((right_now, totals))
        else:
            left_now, _ = lax.optimization_barrier((left_now, right_now))
        waiting.append(arrived)
    far = [(along_ring(my_half(left_now), ring), along_ring(my_half(right_now), ring), half)]
    parts = [(totals[0], wavefunction, 0), (totals[1], sibling_wave, 2)]
    totals = apply_groups(parts, table, waiting, n_sec, n_right)
    (for_sibling,) = apply_groups(
        [(totals[1], sibling_wave, 2)], table, far, n_sec, n_right, jnp.bfloat16
    )
    returned = from_sector(for_sibling, 1)
    (kept,) = apply_groups([(totals[0], wavefunction, 0)], table, far, n_sec, n_right)
    return (kept + returned.astype(jnp.float32)).astype(wavefunction.dtype)


def solution(mesh):
    placed = (
        P(("term", "sector"), None, None),
        P(("term", "sector"), None),
        P(("term", "sector")),
        P("term", "sector", None, None),
        P("term", None, None, None),
    )
    return jax.shard_map(
        local,
        mesh=mesh,
        in_specs=placed,
        out_specs=P(("term", "sector"), None, None),
        check_vma=False,
    )
```

```python
import math

import jax
import jax.numpy as jnp
from jax import lax
from jax.experimental import pallas as pl
from jax.experimental.pallas import tpu as pltpu
from jax.sharding import PartitionSpec as P


def neighbour_ring(n):
    return list(range(0, n, 2)) + list(range(1, n, 2))[::-1]


def along_ring(block, ring):
    n, n_sec = len(ring), lax.axis_size("sector")
    route = []
    for at in range(n):
        for sector in range(n_sec):
            to = (at + (1 if sector % 2 == 0 else -1)) % n
            route.append((ring[at] * n_sec + sector, ring[to] * n_sec + sector))
    return lax.ppermute(block, ("term", "sector"), route)


def from_sector(block, offset):
    n = lax.axis_size("sector")
    return lax.ppermute(block, "sector", [(i, i ^ offset) for i in range(n)])


def apply_groups(parts, table, groups, n_left, n_right, out_dtype=jnp.float32):
    held, order = parts[0][1].shape[:2]
    n_parts, n_groups = len(parts), len(groups)
    fresh = parts[0][0] is None
    together = math.gcd(held, 16)
    terms = [(g, t) for g, group in enumerate(groups) for t in range(group[2])]

    def kernel(*refs):
        table_ref, refs = refs[0], refs[1:]
        group_refs = refs[: n_groups * 2]
        wave_refs = refs[n_groups * 2 : n_groups * 2 + n_parts]
        total_refs = refs[n_groups * 2 + n_parts : -n_parts]
        out_refs = refs[-n_parts:]

        def operator(side, n_slots, g, t, slot):
            ref = group_refs[2 * g + side]
            skip = table_ref[4, 0] if ref.shape[0] > groups[g][2] * n_slots else 0
            return ref[(skip + t) * n_slots + slot]

        def mix(p, first):
            blocks = [first + i for i in range(together)]
            mixed = []
            for k in blocks:
                slot = table_ref[parts[p][2], k]
                lefts = [operator(0, n_left, g, t, slot) for g, t in terms]
                mixed.append(
                    jnp.dot(
                        jnp.concatenate(lefts, axis=0), wave_refs[p][k], preferred_element_type=jnp.float32
                    ).astype(jnp.bfloat16)
                )
            return blocks, mixed

        def finish(p, blocks, mixed):
            added = []
            for k, one in zip(blocks, mixed):
                slot = table_ref[parts[p][2] + 1, k]
                rights = [operator(1, n_right, g, t, slot) for g, t in terms]
                wide = jnp.concatenate(
                    [one[i * order : (i + 1) * order] for i in range(len(terms))], axis=1
                )
                added.append(
                    jnp.dot(wide, jnp.concatenate(rights, axis=0), preferred_element_type=jnp.float32)
                )
            for k, one in zip(blocks, added):
                total = one if fresh else total_refs[p][k] + one
                out_refs[p][k] = total.astype(out_dtype)

        chunks = [(p, *mix(p, first)) for p in range(n_parts) for first in range(0, held, together)]
        for chunk in chunks:
            finish(*chunk)

    smem = pl.BlockSpec(memory_space=pltpu.SMEM)
    vmem = pl.BlockSpec(memory_space=pltpu.VMEM)
    operands = [table] + [x for group in groups for x in group[:2]] + [part[1] for part in parts]
    aliases = {}
    if not fresh:
        if out_dtype == jnp.float32:
            aliases = {len(operands) + p: p for p in range(n_parts)}
        operands += [part[0] for part in parts]
    nbytes = sum(x.size * x.dtype.itemsize for x in operands)
    waves = sum(part[1].size for part in parts)
    return pl.pallas_call(
        kernel,
        out_shape=[jax.ShapeDtypeStruct(part[1].shape, out_dtype) for part in parts],
        in_specs=[smem] + [vmem] * (len(operands) - 1),
        out_specs=[vmem] * n_parts,
        input_output_aliases=aliases,
        compiler_params=pltpu.CompilerParams(vmem_limit_bytes=nbytes + 4 * waves + (16 << 20)),
        cost_estimate=pl.CostEstimate(
            flops=4 * waves * order * len(terms),
            bytes_accessed=nbytes + 4 * waves,
            transcendentals=0,
        ),
    )(*operands)


def local(wavefunction, left_sector, right_sector, left_blocks, right_blocks):
    n_sec = lax.axis_size("sector")
    n_term = lax.axis_size("term")
    order = wavefunction.shape[1]
    held, n_right = right_blocks.shape[:2]
    half = held // 2
    ring = neighbour_ring(n_term)
    sector = lax.axis_index("sector")
    core = sector % 2

    right = jnp.swapaxes(right_blocks, 2, 3).reshape(held * n_right, order, order)
    pair = jnp.concatenate([left_blocks, from_sector(left_blocks, 1)], axis=1)
    others = [from_sector(left_blocks, slot) for slot in range(2, n_sec)]
    pair = lax.optimization_barrier(pair)
    left = jnp.concatenate([pair] + others, axis=1).reshape(held * n_sec, order, order)
    named = jnp.stack([left_sector[:, 0], right_sector])

    def my_half(blocks):
        n = blocks.shape[0] // 2
        return lax.dynamic_slice_in_dim(blocks, core * n, n)

    totals, waiting = (None, None), [(left, right, half)]
    right_now, left_now = right, left
    for turn in range(1, n_term // 2):
        right_now, left_now = along_ring(right_now, ring), along_ring(left_now, ring)
        if turn == 1:
            sent_named, sent_wave, _ = lax.optimization_barrier((named, wavefunction, right_now))
            sibling_named, sibling_wave = from_sector(sent_named, 1), from_sector(sent_wave, 1)
            table = jnp.stack([
                named[0] ^ sector,
                named[1],
                sibling_named[0] ^ sector,
                sibling_named[1],
                jnp.broadcast_to(core * half, named.shape[1:]),
            ])
        arrived = (left_now, right_now, held)
        if turn > 1 and turn % 2 == 1:
            parts = [(totals[0], wavefunction, 0), (totals[1], sibling_wave, 2)]
            totals = apply_groups(parts, table, waiting[:-1], n_sec, n_right)
            waiting = waiting[-1:]
            right_now, totals = lax.optimization_barrier((right_now, totals))
        else:
            left_now, _ = lax.optimization_barrier((left_now, right_now))
        waiting.append(arrived)
    far = [(along_ring(my_half(left_now), ring), along_ring(my_half(right_now), ring), half)]
    parts = [(totals[0], wavefunction, 0), (totals[1], sibling_wave, 2)]
    totals = apply_groups(parts, table, waiting, n_sec, n_right)
    (for_sibling,) = apply_groups(
        [(totals[1], sibling_wave, 2)], table, far, n_sec, n_right, jnp.bfloat16
    )
    returned = from_sector(for_sibling, 1)
    (kept,) = apply_groups([(totals[0], wavefunction, 0)], table, far, n_sec, n_right)
    return (kept + returned.astype(jnp.float32)).astype(wavefunction.dtype)


def solution(mesh):
    placed = (
        P(("term", "sector"), None, None),
        P(("term", "sector"), None),
        P(("term", "sector")),
        P("term", "sector", None, None),
        P("term", None, None, None),
    )
    return jax.shard_map(
        local,
        mesh=mesh,
        in_specs=placed,
        out_specs=P(("term", "sector"), None, None),
        check_vma=False,
    )
```

```python
import math

import jax
import jax.numpy as jnp
from jax import lax
from jax.experimental import pallas as pl
from jax.experimental.pallas import tpu as pltpu
from jax.sharding import PartitionSpec as P


def neighbour_ring(n):
    return list(range(0, n, 2)) + list(range(1, n, 2))[::-1]


def along_ring(block, ring):
    n, n_sec = len(ring), lax.axis_size("sector")
    route = []
    for at in range(n):
        for sector in range(n_sec):
            to = (at + (1 if sector % 2 == 0 else -1)) % n
            route.append((ring[at] * n_sec + sector, ring[to] * n_sec + sector))
    return lax.ppermute(block, ("term", "sector"), route)


def from_sector(block, offset):
    n = lax.axis_size("sector")
    return lax.ppermute(block, "sector", [(i, i ^ offset) for i in range(n)])


def apply_groups(parts, table, groups, n_left, n_right, out_dtype=jnp.float32):
    held, order = parts[0][1].shape[:2]
    n_parts, n_groups = len(parts), len(groups)
    fresh = parts[0][0] is None
    together = math.gcd(held, 16)
    terms = [(g, t) for g, group in enumerate(groups) for t in range(group[2])]

    def kernel(*refs):
        table_ref, refs = refs[0], refs[1:]
        group_refs = refs[: n_groups * 2]
        wave_refs = refs[n_groups * 2 : n_groups * 2 + n_parts]
        total_refs = refs[n_groups * 2 + n_parts : -n_parts]
        out_refs = refs[-n_parts:]

        def operator(side, n_slots, g, t, slot):
            ref = group_refs[2 * g + side]
            skip = table_ref[4, 0] if ref.shape[0] > groups[g][2] * n_slots else 0
            return ref[(skip + t) * n_slots + slot]

        def work_on(p, first):
            blocks = [first + i for i in range(together)]
            mixed = []
            for k in blocks:
                slot = table_ref[parts[p][2], k]
                lefts = [operator(0, n_left, g, t, slot) for g, t in terms]
                mixed.append(
                    jnp.dot(
                        jnp.concatenate(lefts, axis=0), wave_refs[p][k], preferred_element_type=jnp.float32
                    ).astype(jnp.bfloat16)
                )
            added = []
            for k, one in zip(blocks, mixed):
                slot = table_ref[parts[p][2] + 1, k]
                rights = [operator(1, n_right, g, t, slot) for g, t in terms]
                wide = jnp.concatenate(
                    [one[i * order : (i + 1) * order] for i in range(len(terms))], axis=1
                )
                added.append(
                    jnp.dot(wide, jnp.concatenate(rights, axis=0), preferred_element_type=jnp.float32)
                )
            for k, one in zip(blocks, added):
                total = one if fresh else total_refs[p][k] + one
                out_refs[p][k] = total.astype(out_dtype)

        for p in range(n_parts):
            for first in range(0, held, together):
                work_on(p, first)

    smem = pl.BlockSpec(memory_space=pltpu.SMEM)
    vmem = pl.BlockSpec(memory_space=pltpu.VMEM)
    operands = [table] + [x for group in groups for x in group[:2]] + [part[1] for part in parts]
    aliases = {}
    if not fresh:
        if out_dtype == jnp.float32:
            aliases = {len(operands) + p: p for p in range(n_parts)}
        operands += [part[0] for part in parts]
    nbytes = sum(x.size * x.dtype.itemsize for x in operands)
    waves = sum(part[1].size for part in parts)
    return pl.pallas_call(
        kernel,
        out_shape=[jax.ShapeDtypeStruct(part[1].shape, out_dtype) for part in parts],
        in_specs=[smem] + [vmem] * (len(operands) - 1),
        out_specs=[vmem] * n_parts,
        input_output_aliases=aliases,
        compiler_params=pltpu.CompilerParams(vmem_limit_bytes=nbytes + 4 * waves + (8 << 20)),
        cost_estimate=pl.CostEstimate(
            flops=4 * waves * order * len(terms),
            bytes_accessed=nbytes + 4 * waves,
            transcendentals=0,
        ),
    )(*operands)


def local(wavefunction, left_sector, right_sector, left_blocks, right_blocks):
    n_sec = lax.axis_size("sector")
    n_term = lax.axis_size("term")
    order = wavefunction.shape[1]
    held, n_right = right_blocks.shape[:2]
    half = held // 2
    ring = neighbour_ring(n_term)
    sector = lax.axis_index("sector")
    core = sector % 2

    right = jnp.swapaxes(right_blocks, 2, 3).reshape(held * n_right, order, order)
    pair = jnp.concatenate([left_blocks, from_sector(left_blocks, 1)], axis=1)
    others = [from_sector(left_blocks, slot) for slot in range(2, n_sec)]
    pair = lax.optimization_barrier(pair)
    left = jnp.concatenate([pair] + others, axis=1).reshape(held * n_sec, order, order)
    named = jnp.stack([left_sector[:, 0], right_sector])

    def my_half(blocks):
        n = blocks.shape[0] // 2
        return lax.dynamic_slice_in_dim(blocks, core * n, n)

    totals, waiting = (None, None), [(left, right, half)]
    right_now, left_now = right, left
    for turn in range(1, n_term // 2):
        right_now, left_now = along_ring(right_now, ring), along_ring(left_now, ring)
        if turn == 1:
            sent_named, sent_wave, _ = lax.optimization_barrier((named, wavefunction, right_now))
            sibling_named, sibling_wave = from_sector(sent_named, 1), from_sector(sent_wave, 1)
            table = jnp.stack([
                named[0] ^ sector,
                named[1],
                sibling_named[0] ^ sector,
                sibling_named[1],
                jnp.broadcast_to(core * half, named.shape[1:]),
            ])
        arrived = (left_now, right_now, held)
        if turn > 1 and turn % 2 == 1:
            parts = [(totals[0], wavefunction, 0), (totals[1], sibling_wave, 2)]
            totals = apply_groups(parts, table, waiting[:-1], n_sec, n_right)
            waiting = waiting[-1:]
            right_now, totals = lax.optimization_barrier((right_now, totals))
        else:
            left_now, _ = lax.optimization_barrier((left_now, right_now))
        waiting.append(arrived)
    far = [(along_ring(my_half(left_now), ring), along_ring(my_half(right_now), ring), half)]
    parts = [(totals[0], wavefunction, 0), (totals[1], sibling_wave, 2)]
    totals = apply_groups(parts, table, waiting, n_sec, n_right)
    (for_sibling,) = apply_groups(
        [(totals[1], sibling_wave, 2)], table, far, n_sec, n_right, jnp.bfloat16
    )
    returned = jnp.concatenate([from_sector(part, 1) for part in jnp.split(for_sibling, 2)])
    (kept,) = apply_groups([(totals[0], wavefunction, 0)], table, far, n_sec, n_right)
    return (kept + returned.astype(jnp.float32)).astype(wavefunction.dtype)


def solution(mesh):
    placed = (
        P(("term", "sector"), None, None),
        P(("term", "sector"), None),
        P(("term", "sector")),
        P("term", "sector", None, None),
        P("term", None, None, None),
    )
    return jax.shard_map(
        local,
        mesh=mesh,
        in_specs=placed,
        out_specs=P(("term", "sector"), None, None),
        check_vma=False,
    )
```
